256 devices in a mesh: dp: 4 (over x_hi, core), prompt: 16 (over z, x_lo), resp: 4 (over y).
Axes of the slice: x: 4 (x_hi: 2, x_lo: 2; x = x_hi * 2 + x_lo), y: 4, z: 8, core: 2. Of those that a mesh axis runs over, the one named last changes fastest.
Arguments:
- prompt_q: bfloat16 [4096, 4096], P(('prompt', 'resp'), 'dp'), may hold values from -6 to 6
- prompt_key_value: bfloat16 [2, 4096, 512], P(None, ('prompt', 'resp'), 'dp'), may hold values from -6 to 6
- resp_q: bfloat16 [2, 2048, 4096], P(None, ('prompt', 'resp'), 'dp'), may hold values from -6 to 6
- response_key_value: bfloat16 [2, 2, 2048, 512], P(None, None, ('prompt', 'resp'), 'dp'), may hold values from -6 to 6
- labels: int32 [2, 2048], P(None, ('prompt', 'resp')), may hold values 0 or 1
- logp_rest: float32 [2, 2048], P(None, ('prompt', 'resp')), may hold values from -0.75 to 0.75
- resp_probe: bfloat16 [2, 2048, 4096], P(None, ('prompt', 'resp'), 'dp'), may hold values from -0.75 to 0.75
- prompt_probe: bfloat16 [4096, 4096], P(('prompt', 'resp'), 'dp'), may hold values from -6 to 6
Outputs:
- prompt_out: bfloat16 [4096, 4096], P(('prompt', 'resp'), 'dp')
- resp_out: bfloat16 [2, 2048, 4096], P(None, ('prompt', 'resp'), 'dp')
- prompt_dq: bfloat16 [4096, 4096], P(('prompt', 'resp'), 'dp')
- resp_dq: bfloat16 [2, 2048, 4096], P(None, ('prompt', 'resp'), 'dp')
- prompt_dkv: bfloat16 [2, 4096, 512], P(None, ('prompt', 'resp'), 'dp')
- resp_dkv: bfloat16 [2, 2, 2048, 512], P(None, None, ('prompt', 'resp'), 'dp')
- dpo_loss: float32 [], replicated
The draws below stay inside these ranges and needn't reach their ends.
All inputs are finite; a program needn't handle non-finite values. No bound on the sum of `labels` on one device may be relied on, other than what follows from the above.
Results may differ from the reference program's by a relative error of at most 0.039.
Values may be sent and summed in bfloat16 or wider, within the bound.
No kernel may reach another device: no remote copies, remote signals or barrier semaphores. Data moves between devices by JAX's collectives and lax.ppermute only.
A program may use at most 128 MiB of HBM per device.

```python
import jax
import jax.numpy as jnp
from jax import lax

QUERY_HEADS = 32
KEY_VALUE_HEADS = 4
HEAD_SIZE = 128
PROMPT_LENGTH = 4096
RESPONSE_LENGTH = 2048


def draw_prompt_q(key, part):
    key = jax.random.fold_in(key, 11)
    base_sample = jax.random.truncated_normal(key, -6.0, 6.0, (PROMPT_LENGTH, QUERY_HEADS * HEAD_SIZE), jnp.float32)
    return base_sample.astype(jnp.bfloat16)


def draw_resp_q(key, part):
    key = jax.random.fold_in(key, 23)
    base_sample = jax.random.truncated_normal(key, -6.0, 6.0, (2, RESPONSE_LENGTH, QUERY_HEADS * HEAD_SIZE), jnp.float32)
    return base_sample.astype(jnp.bfloat16)


def draw_prompt_key_value(key, part):
    key = jax.random.fold_in(key, 37)
    base_sample = jax.random.truncated_normal(key, -6.0, 6.0, (2, PROMPT_LENGTH, KEY_VALUE_HEADS * HEAD_SIZE), jnp.float32)
    return base_sample.astype(jnp.bfloat16)


def touch_ends(result, key, smallest, high):
    place = [jax.random.randint(jax.random.fold_in(key, axis), (), 0, length) for axis, length in enumerate(result.shape)]
    longest = result.shape.index(max(result.shape))
    neighbour = place[:longest] + [(place[longest] + 1) % result.shape[longest]] + place[longest + 1:]
    return result.at[tuple(place)].set(smallest).at[tuple(neighbour)].set(high)


def block_levels(stream_key, extent, cuts, least, top_value):
    loudness = 1.0
    for dim, blocks in cuts:
        steps = jax.random.uniform(jax.random.fold_in(jax.random.fold_in(stream_key, 6), dim), (blocks,), jnp.float32, least / len(cuts), top_value / len(cuts))
        loudness = loudness * jnp.repeat(jnp.exp(steps), extent[dim] // blocks).reshape((-1,) + (1,) * (len(extent) - 1 - dim))
    return loudness


def bell_draw(own_key, dims, scale, bound, cuts=(), kind=jnp.bfloat16):
    entries = scale * jax.random.normal(own_key, dims, jnp.float32)
    if cuts:
        entries = entries * block_levels(own_key, dims, cuts, -0.22, 0.18)
    return jnp.clip(entries, -bound, bound).astype(kind)


def setup_inputs(seed: int = 0) -> dict:
    key_list = jax.random.split(jax.random.key(seed), 9)
    return {
        "prompt_q": draw_prompt_q(jax.random.fold_in(key_list[8], 71), 0),
        "prompt_key_value": draw_prompt_key_value(jax.random.fold_in(key_list[8], 71), 0),
        "resp_q": draw_resp_q(jax.random.fold_in(key_list[8], 71), 0),
        "response_key_value": bell_draw(key_list[3], (2, 2, RESPONSE_LENGTH, KEY_VALUE_HEADS * HEAD_SIZE), 1.0, 6.0, ((2, 64), (3, 4))),
        "labels": touch_ends((jax.random.randint(key_list[4], (2, RESPONSE_LENGTH), 0, 8) < 7).astype(jnp.int32), jax.random.fold_in(key_list[4], 1), 0, 1),
        "logp_rest": bell_draw(key_list[5], (2, RESPONSE_LENGTH), 0.05, 0.75, ((1, 64),), jnp.float32),
        "resp_probe": bell_draw(key_list[6], (2, RESPONSE_LENGTH, QUERY_HEADS * HEAD_SIZE), 0.05, 0.75, ((1, 64), (2, 4))),
        "prompt_probe": bell_draw(key_list[7], (PROMPT_LENGTH, QUERY_HEADS * HEAD_SIZE), 1.0, 6.0, ((0, 64), (1, 4))),
    }


NEG_FILL = -1e+30
BETA = 0.1

def probabilities(queries, key_rows, visible):
    softmax_scale = queries.shape[-1] ** (-0.5)
    raw_scores = jnp.dot(queries, key_rows.T, preferred_element_type=jnp.float32) * softmax_scale
    masked = jnp.where(visible, raw_scores, NEG_FILL)
    peak_score = lax.optimization_barrier(jnp.max(masked, axis=1, keepdims=True))
    log_total = peak_score + jnp.log(lax.optimization_barrier(jnp.sum(jnp.exp(masked - peak_score), axis=1, keepdims=True)))
    return jnp.exp(masked - log_total)

def attend(queries, key_rows, value_rows, visible):
    prob_full = probabilities(queries, key_rows, visible)
    return jnp.dot(prob_full.astype(jnp.bfloat16), value_rows, preferred_element_type=jnp.float32).astype(jnp.bfloat16)

def attend_grad(queries, key_rows, value_rows, visible, outputs, grad_out):
    softmax_scale = queries.shape[-1] ** (-0.5)
    prob_full = probabilities(queries, key_rows, visible)
    weights = prob_full.astype(jnp.bfloat16)
    dprob_full = jnp.dot(grad_out, value_rows.T, preferred_element_type=jnp.float32)
    row_delta = lax.optimization_barrier(jnp.sum(grad_out.astype(jnp.float32) * outputs.astype(jnp.float32), axis=1, keepdims=True))
    dscore = (prob_full * (dprob_full - row_delta)).astype(jnp.bfloat16)
    dquery = (jnp.dot(dscore, key_rows, preferred_element_type=jnp.float32) * softmax_scale).astype(jnp.bfloat16)
    dkey_rows = jnp.dot(dscore.T, queries, preferred_element_type=jnp.float32) * softmax_scale
    dvalue = jnp.dot(weights.T, grad_out, preferred_element_type=jnp.float32)
    return (dquery, dkey_rows, dvalue)

def reference(prompt_q, prompt_key_value, resp_q, response_key_value, labels, logp_rest, resp_probe, prompt_probe):
    query_groups = QUERY_HEADS // KEY_VALUE_HEADS
    prompt_grand_sum = PROMPT_LENGTH
    response_grand_sum = RESPONSE_LENGTH
    head_pq = prompt_q.reshape(prompt_grand_sum, QUERY_HEADS, HEAD_SIZE).transpose(1, 0, 2)
    head_rq = resp_q.reshape(2, response_grand_sum, QUERY_HEADS, HEAD_SIZE).transpose(2, 0, 1, 3)
    head_prompt_key = jnp.repeat(prompt_key_value[0].reshape(prompt_grand_sum, KEY_VALUE_HEADS, HEAD_SIZE).transpose(1, 0, 2), query_groups, axis=0)
    head_prompt_value = jnp.repeat(prompt_key_value[1].reshape(prompt_grand_sum, KEY_VALUE_HEADS, HEAD_SIZE).transpose(1, 0, 2), query_groups, axis=0)
    head_response_key = jnp.repeat(response_key_value[0].reshape(2, response_grand_sum, KEY_VALUE_HEADS, HEAD_SIZE).transpose(2, 0, 1, 3), query_groups, axis=0)
    head_response_value = jnp.repeat(response_key_value[1].reshape(2, response_grand_sum, KEY_VALUE_HEADS, HEAD_SIZE).transpose(2, 0, 1, 3), query_groups, axis=0)
    prompt_pos = jnp.arange(prompt_grand_sum, dtype=jnp.int32)
    prompt_visible = prompt_pos[:, None] >= prompt_pos[None, :]
    key_index = jnp.arange(prompt_grand_sum + response_grand_sum, dtype=jnp.int32)
    resp_pos = jnp.arange(response_grand_sum, dtype=jnp.int32)
    resp_visible = (key_index[None, :] < prompt_grand_sum) | (key_index[None, :] - prompt_grand_sum <= resp_pos[:, None])

    def forward_head(head_items):
        q_prompt, q_resp, k_prompt, v_prompt, k_resp, v_resp = head_items
        out_prompt = attend(q_prompt, k_prompt, v_prompt, prompt_visible)
        out_resp = jnp.stack([attend(q_resp[side_index], jnp.concatenate([k_prompt, k_resp[side_index]], axis=0), jnp.concatenate([v_prompt, v_resp[side_index]], axis=0), resp_visible) for side_index in range(2)])
        return (out_prompt, out_resp)
    out_prompt, out_resp = lax.map(forward_head, (head_pq, head_rq, head_prompt_key, head_prompt_value, head_response_key, head_response_value))
    prompt_out = out_prompt.transpose(1, 0, 2).reshape(prompt_grand_sum, QUERY_HEADS * HEAD_SIZE)
    resp_out = out_resp.transpose(1, 2, 0, 3).reshape(2, response_grand_sum, QUERY_HEADS * HEAD_SIZE)
    sign_row = jnp.array([1.0, -1.0], dtype=jnp.float32)
    counted = labels.astype(jnp.float32) * sign_row[:, None]
    probe_score = lax.optimization_barrier(jnp.sum(resp_out.astype(jnp.float32) * resp_probe.astype(jnp.float32), axis=-1))
    margin = BETA * jnp.sum(counted * (logp_rest + probe_score))
    dpo_loss = jax.nn.softplus(-margin)
    weight = -BETA * jax.nn.sigmoid(-margin)
    resp_grad = ((weight * counted)[..., None] * resp_probe.astype(jnp.float32)).astype(jnp.bfloat16)
    prompt_grad = (weight * prompt_probe.astype(jnp.float32)).astype(jnp.bfloat16)
    head_rg = resp_grad.reshape(2, response_grand_sum, QUERY_HEADS, HEAD_SIZE).transpose(2, 0, 1, 3)
    head_pg = prompt_grad.reshape(prompt_grand_sum, QUERY_HEADS, HEAD_SIZE).transpose(1, 0, 2)

    def backward_head(head_items):
        q_prompt, q_resp, k_prompt, v_prompt, k_resp, v_resp, o_prompt, o_resp, g_prompt, g_resp = head_items
        dq_prompt, dk_prompt, dv_prompt = attend_grad(q_prompt, k_prompt, v_prompt, prompt_visible, o_prompt, g_prompt)
        dq_list = []
        dk_list = []
        dv_list = []
        for side_index in range(2):
            dq_side, dk_side, dv_side = attend_grad(q_resp[side_index], jnp.concatenate([k_prompt, k_resp[side_index]], axis=0), jnp.concatenate([v_prompt, v_resp[side_index]], axis=0), resp_visible, o_resp[side_index], g_resp[side_index])
            dk_prompt = dk_prompt + dk_side[:prompt_grand_sum]
            dv_prompt = dv_prompt + dv_side[:prompt_grand_sum]
            dq_list.append(dq_side)
            dk_list.append(dk_side[prompt_grand_sum:])
            dv_list.append(dv_side[prompt_grand_sum:])
        return (dq_prompt, jnp.stack(dq_list), dk_prompt, dv_prompt, jnp.stack(dk_list), jnp.stack(dv_list))
    dq_prompt, dq_resp, dk_prompt, dv_prompt, dk_resp, dv_resp = lax.map(backward_head, (head_pq, head_rq, head_prompt_key, head_prompt_value, head_response_key, head_response_value, out_prompt, out_resp, head_pg, head_rg))
    prompt_dq = dq_prompt.transpose(1, 0, 2).reshape(prompt_grand_sum, QUERY_HEADS * HEAD_SIZE)
    resp_dq = dq_resp.transpose(1, 2, 0, 3).reshape(2, response_grand_sum, QUERY_HEADS * HEAD_SIZE)

    def prompt_fold(gradient_list):
        reduced_sum = gradient_list.reshape(KEY_VALUE_HEADS, query_groups, prompt_grand_sum, HEAD_SIZE).sum(axis=1)
        return reduced_sum.transpose(1, 0, 2).reshape(prompt_grand_sum, KEY_VALUE_HEADS * HEAD_SIZE)

    def resp_fold(gradient_list):
        reduced_sum = gradient_list.reshape(KEY_VALUE_HEADS, query_groups, 2, response_grand_sum, HEAD_SIZE).sum(axis=1)
        return reduced_sum.transpose(1, 2, 0, 3).reshape(2, response_grand_sum, KEY_VALUE_HEADS * HEAD_SIZE)
    prompt_dkv = jnp.stack([prompt_fold(dk_prompt), prompt_fold(dv_prompt)]).astype(jnp.bfloat16)
    resp_dkv = jnp.stack([resp_fold(dk_resp), resp_fold(dv_resp)]).astype(jnp.bfloat16)
    return (prompt_out, resp_out, prompt_dq, resp_dq, prompt_dkv, resp_dkv, dpo_loss)
```

```python
import functools
import math

import jax
import jax.numpy as jnp
from jax import lax
from jax.experimental import pallas as pl
from jax.experimental.pallas import tpu as pltpu
from jax.sharding import PartitionSpec as P

QUERY_HEADS = 32
KEY_VALUE_HEADS = 4
HEAD_SIZE = 128
BETA = 0.1
HIDDEN = -1e30
FLOOR = -1e29
SCALE = HEAD_SIZE ** -0.5
SCALE2 = SCALE * math.log2(math.e)

HEADS = QUERY_HEADS // KEY_VALUE_HEADS
D = HEAD_SIZE
BF16 = jnp.bfloat16
F32 = jnp.float32
CHUNK = 256

NT = (((1,), (1,)), ((), ()))
TN = (((0,), (0,)), ((), ()))
NN = (((1,), (0,)), ((), ()))


def mm(a, b, dims):
    return lax.dot_general(a, b, dims, preferred_element_type=F32)


def counted_rows(labels):
    row = lax.broadcasted_iota(jnp.int32, labels.shape, 0)
    return labels.astype(F32) * jnp.where(row == 0, 1.0, -1.0)


def as_column(row):
    n = row.shape[1]
    r = lax.broadcasted_iota(jnp.int32, (n, n), 0)
    c = lax.broadcasted_iota(jnp.int32, (n, n), 1)
    return jnp.sum(jnp.where(r == c, jnp.broadcast_to(row, (n, n)), 0.0), axis=1, keepdims=True)


def pack_kernel(sizes, pq, pkv, rq, rkv, labels, probe, pprobe, qg, kvb):
    tp, tr, groups = sizes
    qg[0:tp] = pq[...]
    qg[tp + 2 * tr : 2 * tp + 2 * tr] = pprobe[...]
    counted = counted_rows(labels[...])
    for s in range(2):
        qg[tp + s * tr : tp + (s + 1) * tr] = rq[s]
        col = as_column(counted[s : s + 1])
        base = 2 * tp + 2 * tr + s * tr
        qg[base : base + tr] = (probe[s].astype(F32) * col).astype(BF16)
    for g in range(groups):
        for i in range(2):
            kvb[g, i * tp : (i + 1) * tp] = pkv[i]
            for s in range(2):
                base = 2 * tp + (2 * i + s) * tr
                kvb[g, base : base + tr] = rkv[i, s]


def tile_lanes(sizes, ways):
    tp, tr, _ = sizes
    half = ways // 2
    return [(0, 0, ways), (1, 0, ways), (-1, 0, half), (-1, half, ways)]


def limits(kind, first, last, rows, g, y):
    lanes = (last - first) * HEADS * rows
    lane = lax.broadcasted_iota(jnp.int32, (1, lanes), 1)
    src = first + lane // (HEADS * rows)
    t = lane % rows
    return g * rows + jnp.where(src == 0, t + 1, jnp.where(src > y, rows, 0))


def hide(s, start, lim):
    key = lax.broadcasted_iota(jnp.int32, s.shape, 0) + start
    return jnp.where(key < lim, s, HIDDEN)


def key_chunk(kv, chunk, rows, base):
    n = CHUNK // rows
    return kv[pl.ds(chunk * n, n), base : base + rows, :].reshape(CHUNK, D)


def offsets(kind, sizes):
    tp, tr, _ = sizes
    if kind < 0:
        return 0, tp
    return 2 * tp + kind * tr, 2 * tp + 2 * tr + kind * tr


def row_base(kind, sizes, ways):
    tp, tr, _ = sizes
    return 0 if kind < 0 else ways * HEADS * (tp + kind * tr)


def stats_lane(kind, sizes):
    tp, tr, _ = sizes
    return 0 if kind < 0 else HEADS * (tp + kind * tr)


def forward_kernel(sizes, ways, where, labels, logp, kv, *refs):
    qg = refs[:ways]
    qs, gs, ot, stats, s_scr = refs[ways:]
    tp, tr, groups = sizes
    g, y = where[0], where[1]
    counted = counted_rows(labels[...])
    rest = jnp.sum(counted * logp[...], axis=(0, 1), keepdims=True)

    for tile, (kind, first, last) in enumerate(tile_lanes(sizes, ways)):
        rows = tp if kind < 0 else tr
        qrow = 0 if kind < 0 else tp + kind * tr
        grow = qrow + tp + 2 * tr
        per = HEADS * rows
        lanes = (last - first) * per
        base = row_base(kind, sizes, ways) + first * per
        for j in range(first, last):
            for h in range(HEADS):
                at = base + (j - first) * per + h * rows
                qs[at : at + rows] = qg[j][qrow : qrow + rows, h * D : (h + 1) * D]
                gs[at : at + rows] = qg[j][grow : grow + rows, h * D : (h + 1) * D]
        q = qs[base : base + lanes]
        grad = gs[base : base + lanes]
        lim = limits(kind, first, last, rows, g, y)
        koff, voff = offsets(kind, sizes)
        n_prompt = groups * tp // CHUNK if kind >= 0 else 0
        per_chunk = CHUNK // rows
        n_own = g // per_chunk + 1

        def score_step(chunk, peak, rows_k, off, start, lim, masked):
            s = mm(key_chunk(kv, chunk, rows_k, off), q, NT) * SCALE2
            if masked:
                s = hide(s, chunk * CHUNK, lim)
            s_scr[pl.ds(start + chunk * CHUNK, CHUNK), :] = s
            return jnp.maximum(peak, jnp.max(s.reshape(CHUNK // 8, 8, lanes), axis=0))

        peak = jnp.full((8, lanes), FLOOR, F32)
        if n_prompt:
            peak = lax.fori_loop(
                0, n_prompt, lambda c, p: score_step(c, p, tp, 0, 0, None, False), peak
            )
        skip = n_prompt * CHUNK
        peak = lax.fori_loop(
            0, n_own, lambda c, p: score_step(c, p, rows, koff, skip, lim, True), peak
        )
        peak = jnp.max(peak, axis=0, keepdims=True)
        ot[tile] = jnp.zeros((D, lanes), F32)

        def out_step(chunk, sums, rows_k, off, start):
            total, dots = sums
            v = key_chunk(kv, chunk, rows_k, off)
            p = jnp.exp2(s_scr[pl.ds(start + chunk * CHUNK, CHUNK), :] - peak)
            dp = mm(v, grad, NT)
            total = total + jnp.sum(p.reshape(CHUNK // 8, 8, lanes), axis=0)
            dots = dots + jnp.sum((p * dp).reshape(CHUNK // 8, 8, lanes), axis=0)
            ot[tile] += mm(v, p.astype(BF16), TN)
            return total, dots

        sums = (jnp.zeros((8, lanes), F32), jnp.zeros((8, lanes), F32))
        if n_prompt:
            sums = lax.fori_loop(
                0, n_prompt, lambda c, s: out_step(c, s, tp, tp, 0), sums
            )
        sums = lax.fori_loop(0, n_own, lambda c, s: out_step(c, s, rows, voff, skip), sums)
        total = jnp.sum(sums[0], axis=0, keepdims=True)
        dots = jnp.sum(sums[1], axis=0, keepdims=True)
        lane0 = stats_lane(kind, sizes)
        for j in range(first, last):
            a = (j - first) * per
            for k, v in enumerate((peak, total, dots)):
                stats[j, k : k + 1, lane0 : lane0 + per] = v[:, a : a + per]
            stats[j, 3:4, lane0 : lane0 + per] = jnp.broadcast_to(rest, (1, per))


def combine_kernel(sizes, ways, copies, *refs):
    got = refs[:ways]
    out, margin = refs[ways:]
    tp, tr, _ = sizes
    acc = jnp.zeros((1, 1), F32)
    for i in range(ways):
        parts = [got[j][(i - j) % ways] for j in range(ways)]
        peak = functools.reduce(jnp.maximum, [p[0:1] for p in parts])
        scales = [jnp.exp2(p[0:1] - peak) for p in parts]
        total = sum(s * p[1:2] for s, p in zip(scales, parts))
        dots = sum(s * p[2:3] for s, p in zip(scales, parts))
        delta = dots / total
        out[0, i : i + 1] = peak + jnp.log2(total)
        out[1, i : i + 1] = delta
        out[2, i : i + 1] = scales[0] / total
        acc = acc + jnp.sum(delta[:, HEADS * tp :], axis=1, keepdims=True)
    rest = sum(got[j][0, 3:4, 0:1] for j in range(ways)) / copies
    margin[...] = jnp.broadcast_to(BETA * (acc + rest), margin.shape)


def backward_kernel(sizes, ways, where, kv, qs, gs, ot, info, *refs):
    odq, (dkv, acc, dqt) = refs[:ways], refs[ways:]
    tp, tr, groups = sizes
    g, y = where[0], where[1]
    acc[...] = jnp.zeros(acc.shape, F32)

    for tile, (kind, first, last) in enumerate(tile_lanes(sizes, ways)):
        rows = tp if kind < 0 else tr
        qrow = 0 if kind < 0 else tp + kind * tr
        grow = qrow + tp + 2 * tr
        per = HEADS * rows
        lanes = (last - first) * per
        base = row_base(kind, sizes, ways) + first * per
        q = qs[base : base + lanes]
        grad = gs[base : base + lanes]
        lim = limits(kind, first, last, rows, g, y)
        koff, voff = offsets(kind, sizes)
        lane0 = stats_lane(kind, sizes)
        lse, delta, alpha = (
            jnp.concatenate(
                [info[k, j : j + 1, lane0 : lane0 + per] for j in range(first, last)], axis=1
            )
            for k in range(3)
        )
        n_prompt = groups * tp // CHUNK if kind >= 0 else 0
        n_own = g // (CHUNK // rows) + 1
        dqt[...] = jnp.zeros((D, lanes), F32)

        def step(chunk, rows_k, ko, vo, masked):
            n = CHUNK // rows_k
            k = key_chunk(kv, chunk, rows_k, ko)
            v = key_chunk(kv, chunk, rows_k, vo)
            s = mm(k, q, NT) * SCALE2 - lse
            if masked:
                s = hide(s, chunk * CHUNK, lim)
            p = jnp.exp2(s)
            ds = (p * (mm(v, grad, NT) - delta)).astype(BF16)
            blocks = pl.ds(chunk * n, n)
            acc[blocks, vo : vo + rows_k, :] += mm(p.astype(BF16), grad, NN).reshape(n, rows_k, D)
            acc[blocks, ko : ko + rows_k, :] += mm(ds, q, NN).reshape(n, rows_k, D)
            dqt[...] += mm(k, ds, TN)

        if n_prompt:
            pl.loop(0, n_prompt)(lambda c: step(c, tp, 0, tp, False))
        pl.loop(0, n_own)(lambda c: step(c, rows, koff, voff, True))

        for half, whole in ((0, ot[tile] * alpha), (tp + 2 * tr, dqt[...])):
            turned = whole.T.astype(BF16)
            for j in range(first, last):
                for h in range(HEADS):
                    at = (j - first) * per + h * rows
                    odq[j][qrow + half : qrow + half + rows, h * D : (h + 1) * D] = turned[
                        at : at + rows
                    ]
    dkv[:, 0 : 2 * tp + 4 * tr, :] = acc[...].astype(BF16)
    dkv[:, 2 * tp + 4 * tr :, :] = jnp.zeros((groups, 16, D), BF16)


def final_kernel(sizes, ways, terms, mine, *refs):
    others = refs[: ways - 1]
    p_out, r_out, p_dq, r_dq, p_dkv, r_dkv, loss = refs[ways - 1 :]
    tp, tr, groups = sizes
    n = 2 * tp + 4 * tr
    parts = jnp.sum(terms[:, n : n + 16, :].astype(F32), axis=0)
    margin = jnp.sum(parts[0:8], axis=0, keepdims=True)
    z = -margin
    loss[...] = jnp.maximum(z, 0.0) + jnp.log1p(jnp.exp(-jnp.abs(z)))
    weight = -BETA / (1.0 + jnp.exp(margin))
    weight = weight[:, 0:1]

    def gathered(a, b):
        return mine[a:b].astype(F32) + sum(o[a:b].astype(F32) for o in others)

    half = tp + 2 * tr
    p_out[...] = gathered(0, tp).astype(BF16)
    p_dq[...] = (gathered(half, half + tp) * (weight * SCALE)).astype(BF16)
    for s in range(2):
        a = tp + s * tr
        r_out[s] = gathered(a, a + tr).astype(BF16)
        r_dq[s] = (gathered(half + a, half + a + tr) * (weight * SCALE)).astype(BF16)

    def summed(a, b, scale):
        return (jnp.sum(terms[:, a:b, :].astype(F32), axis=0) * scale).astype(BF16)

    for i, scale in enumerate((weight * SCALE, weight)):
        p_dkv[i] = summed(i * tp, (i + 1) * tp, scale)
        for s in range(2):
            a = 2 * tp + (2 * i + s) * tr
            r_dkv[i, s] = summed(a, a + tr, scale)


VMEM = pl.BlockSpec(memory_space=pltpu.VMEM)
SMEM = pl.BlockSpec(memory_space=pltpu.SMEM)


def call(body, out_shape, ins, scratch=(), limit=56, cost=None):
    return pl.pallas_call(
        body,
        out_shape=out_shape,
        in_specs=ins,
        out_specs=jax.tree.map(lambda _: VMEM, out_shape),
        scratch_shapes=list(scratch),
        cost_estimate=cost,
        compiler_params=pltpu.CompilerParams(vmem_limit_bytes=limit * 1024 * 1024),
    )


def shift(x, axis, by):
    n = lax.axis_size(axis)
    return lax.ppermute(x, axis, [(i, (i + by) % n) for i in range(n)])


def per_device(pq, pkv, rq, rkv, labels, logp, probe, pprobe):
    tp, tr = pq.shape[0], rq.shape[1]
    groups, ways = lax.axis_size("prompt"), lax.axis_size("resp")
    copies = lax.axis_size("dp")
    sizes = (tp, tr, groups)
    wide = HEADS * D
    n = 2 * tp + 4 * tr
    half = tp + 2 * tr
    lanes = HEADS * half
    sds = jax.ShapeDtypeStruct
    where = jnp.stack([lax.axis_index("prompt"), lax.axis_index("resp")]).astype(jnp.int32)

    qg, kvb = call(
        functools.partial(pack_kernel, sizes),
        (sds((2 * half, wide), BF16), sds((groups, n, D), BF16)),
        [VMEM] * 7,
    )(pq, pkv, rq, rkv, labels, probe, pprobe)
    qgs = [qg] + [shift(qg, "resp", j) for j in range(1, ways)]
    kv = lax.all_to_all(kvb, "prompt", 0, 0, tiled=True)

    tiles = len(tile_lanes(sizes, ways))
    tile = ways * lanes // tiles
    qs, gs, ot, stats = call(
        functools.partial(forward_kernel, sizes, ways),
        (
            sds((ways * lanes, D), BF16),
            sds((ways * lanes, D), BF16),
            sds((tiles, D, tile), F32),
            sds((ways, 4, lanes), F32),
        ),
        [SMEM] + [VMEM] * (3 + ways),
        [pltpu.VMEM((groups * (tp + tr), tile), F32)],
        cost=pl.CostEstimate(flops=4_000_000_000, bytes_accessed=8_000_000, transcendentals=0),
    )(where, labels, logp, kv, *qgs)
    all_stats = [stats] + [shift(stats, "resp", j) for j in range(1, ways)]
    info, margin = call(
        functools.partial(combine_kernel, sizes, ways, copies),
        (sds((3, ways, lanes), F32), sds((8, D), F32)),
        [VMEM] * ways,
    )(*all_stats)
    margins = [margin] + [shift(margin, "dp", j) for j in range(1, copies)]

    *odq, dkv = call(
        functools.partial(backward_kernel, sizes, ways),
        (*[sds((2 * half, wide), BF16)] * ways, sds((groups, n + 16, D), BF16)),
        [SMEM] + [VMEM] * 5,
        [pltpu.VMEM((groups, n, D), F32), pltpu.VMEM((D, tile), F32)],
        cost=pl.CostEstimate(flops=7_000_000_000, bytes_accessed=10_000_000, transcendentals=0),
    )(where, kv, qs, gs, ot, info)

    whole = sum(margins)[0:1]
    hi = whole.astype(BF16)
    left = whole - hi.astype(F32)
    mid = left.astype(BF16)
    low = (left - mid.astype(F32)).astype(BF16)
    row = jnp.concatenate([hi, mid, low, jnp.zeros((13, D), BF16)], axis=0)
    dkv = lax.dynamic_update_slice(
        dkv, jnp.broadcast_to(row[None], (groups, 16, D)), (0, n, 0)
    )
    others = [shift(odq[j], "resp", -j) for j in range(1, ways)]
    terms = lax.all_to_all(dkv, "prompt", 0, 0, tiled=True)

    outs = call(
        functools.partial(final_kernel, sizes, ways),
        (
            sds(pq.shape, BF16),
            sds(rq.shape, BF16),
            sds(pq.shape, BF16),
            sds(rq.shape, BF16),
            sds(pkv.shape, BF16),
            sds(rkv.shape, BF16),
            sds((1, D), F32),
        ),
        [VMEM] * (1 + ways),
    )(terms, odq[0], *others)
    return (*outs[:6], outs[6][0, 0])


def solution(mesh):
    placed = (
        P(("prompt", "resp"), "dp"),
        P(None, ("prompt", "resp"), "dp"),
        P(None, ("prompt", "resp"), "dp"),
        P(None, None, ("prompt", "resp"), "dp"),
        P(None, ("prompt", "resp")),
        P(None, ("prompt", "resp")),
        P(None, ("prompt", "resp"), "dp"),
        P(("prompt", "resp"), "dp"),
    )
    return jax.shard_map(
        per_device,
        mesh=mesh,
        in_specs=placed,
        out_specs=(
            P(("prompt", "resp"), "dp"),
            P(None, ("prompt", "resp"), "dp"),
            P(("prompt", "resp"), "dp"),
            P(None, ("prompt", "resp"), "dp"),
            P(None, ("prompt", "resp"), "dp"),
            P(None, None, ("prompt", "resp"), "dp"),
            P(),
        ),
        check_vma=False,
    )
```

```python
import functools
import math

import jax
import jax.numpy as jnp
from jax import lax
from jax.experimental import pallas as pl
from jax.experimental.pallas import tpu as pltpu
from jax.sharding import PartitionSpec as P

QUERY_HEADS = 32
KEY_VALUE_HEADS = 4
HEAD_SIZE = 128
BETA = 0.1
HIDDEN = -1e30
FLOOR = -1e29
SCALE = HEAD_SIZE ** -0.5
SCALE2 = SCALE * math.log2(math.e)

HEADS = QUERY_HEADS // KEY_VALUE_HEADS
D = HEAD_SIZE
BF16 = jnp.bfloat16
F32 = jnp.float32
CHUNK = 512

NT = (((1,), (1,)), ((), ()))
TN = (((0,), (0,)), ((), ()))
NN = (((1,), (0,)), ((), ()))


def mm(a, b, dims):
    return lax.dot_general(a, b, dims, preferred_element_type=F32)


def counted_rows(labels):
    row = lax.broadcasted_iota(jnp.int32, labels.shape, 0)
    return labels.astype(F32) * jnp.where(row == 0, 1.0, -1.0)


def as_column(row):
    n = row.shape[1]
    r = lax.broadcasted_iota(jnp.int32, (n, n), 0)
    c = lax.broadcasted_iota(jnp.int32, (n, n), 1)
    return jnp.sum(jnp.where(r == c, jnp.broadcast_to(row, (n, n)), 0.0), axis=1, keepdims=True)


def pack_kernel(sizes, pq, pkv, rq, rkv, labels, logp, probe, pprobe, *refs):
    qg, kvb, rest, kv_in, rkv_in, labels_in, logp_in, probe_in, sems = refs
    tp, tr, groups = sizes
    half = tp + 2 * tr
    moves = [
        (pkv, kv_in),
        (rkv, rkv_in),
        (labels, labels_in),
        (probe, probe_in),
        (logp, logp_in),
        (pq, qg.at[0:tp]),
        (rq.at[0], qg.at[tp : tp + tr]),
        (rq.at[1], qg.at[tp + tr : half]),
        (pprobe, qg.at[half : half + tp]),
    ]
    copies = [pltpu.make_async_copy(a, b, sems.at[i]) for i, (a, b) in enumerate(moves)]
    for copy in copies:
        copy.start()
    copies[0].wait()
    copies[1].wait()
    for g in range(groups):
        for i in range(2):
            kvb[g, i * tp : (i + 1) * tp] = kv_in[i]
            for s in range(2):
                base = 2 * tp + (2 * i + s) * tr
                kvb[g, base : base + tr] = rkv_in[i, s]
    copies[2].wait()
    copies[3].wait()
    counted = counted_rows(labels_in[...])
    for s in range(2):
        col = as_column(counted[s : s + 1])
        base = half + tp + s * tr
        qg[base : base + tr] = (probe_in[s].astype(F32) * col).astype(BF16)
    copies[4].wait()
    rest[...] = jnp.broadcast_to(
        jnp.sum(counted * logp_in[...], axis=(0, 1), keepdims=True), rest.shape
    )
    for copy in copies[5:]:
        copy.wait()


def key_rows(kv, rows, base, chunk):
    n = CHUNK // rows
    return kv[chunk * n : (chunk + 1) * n, base : base + rows, :].reshape(CHUNK, D)


def limits(rows, slot):
    g, y = lax.axis_index("prompt"), lax.axis_index("resp")
    if slot == 0:
        lane = lax.broadcasted_iota(jnp.int32, (1, HEADS * rows), 1)
        return g * rows + lane % rows + 1
    return jnp.full((1, HEADS * rows), g * rows + jnp.where(slot > y, rows, 0), jnp.int32)


def hide(s, start, lim):
    key = lax.broadcasted_iota(jnp.int32, s.shape, 0) + start
    return jnp.where(key < lim, s, HIDDEN)


def pieces(sizes):
    tp, tr, _ = sizes
    half = tp + 2 * tr
    out = [(tp, 0, 0, 0, tp)]
    for s in range(2):
        out.append((tr, HEADS * (tp + s * tr), tp + s * tr, 2 * tp + s * tr, 2 * tp + (2 + s) * tr))
    return out


def steps(sizes):
    tp, tr, groups = sizes
    full = HEADS * (tp + 2 * tr)
    out = [(0, c, 0, full, 0, HEADS * tp) for c in range(groups * tp // CHUNK)]
    for kind, (rows, lane, *_) in enumerate(pieces(sizes)):
        if kind:
            wide = HEADS * rows
            out += [(kind, c, lane, lane + wide, lane, lane + wide) for c in range(groups * rows // CHUNK)]
    return out


def scores(kv, q, sizes, step, lim):
    kind, chunk, a, b, ma, mb = step
    rows, _, _, koff, _ = pieces(sizes)[kind]
    s = mm(key_rows(kv, rows, koff, chunk), q[a:b], NT)
    shown = hide(s[:, : mb - ma], chunk * CHUNK, lim[kind])
    return shown if mb == b else jnp.concatenate([shown, s[:, mb - ma :]], axis=1)


def forward_kernel(sizes, slot, kv, qg, *refs):
    if slot == 0:
        rest, qs, gs, ot, stats, s_scr = refs
        stats[...] = jnp.zeros(stats.shape, F32)
    else:
        _, qs, gs, ot, stats, s_scr = refs
    tp, tr, groups = sizes
    half = tp + 2 * tr
    lanes = HEADS * half
    for rows, lane, row, _, _ in pieces(sizes):
        for h in range(HEADS):
            at = lane + h * rows
            qs[at : at + rows] = qg[row : row + rows, h * D : (h + 1) * D]
            gs[at : at + rows] = qg[half + row : half + row + rows, h * D : (h + 1) * D]
    lim = [limits(p[0], slot) for p in pieces(sizes)]
    todo = steps(sizes)

    peak = jnp.full((8, lanes), FLOOR, F32)
    for i, step in enumerate(todo):
        a, b = step[2:4]
        s = scores(kv, qs, sizes, step, lim)
        s_scr[i * CHUNK : (i + 1) * CHUNK, a:b] = s
        top = jnp.max(s.reshape(CHUNK // 8, 8, b - a), axis=0)
        peak = jnp.maximum(peak, top) if b - a == lanes else over(peak, top, a, b, jnp.maximum)
    peak = jnp.max(peak, axis=0, keepdims=True) * SCALE2

    total = jnp.zeros((8, lanes), F32)
    out = jnp.zeros((D, lanes), F32)
    for i, step in enumerate(todo):
        kind, chunk, a, b = step[:4]
        rows, _, _, _, voff = pieces(sizes)[kind]
        p = jnp.exp2(s_scr[i * CHUNK : (i + 1) * CHUNK, a:b] * SCALE2 - peak[:, a:b])
        part = mm(key_rows(kv, rows, voff, chunk), p.astype(BF16), TN)
        out = over(out, part, a, b, jnp.add)
        total = over(total, jnp.sum(p.reshape(CHUNK // 8, 8, b - a), axis=0), a, b, jnp.add)
    total = jnp.sum(total, axis=0, keepdims=True)
    ot[...] = out
    dots = jnp.sum(out * gs[...].astype(F32).T, axis=0, keepdims=True)
    stats[slot, 0:1] = peak
    stats[slot, 1:2] = total
    stats[slot, 2:3] = dots
    if slot == 0:
        stats[slot, 3:4, 0:D] = rest[0:1]


def over(whole, part, a, b, op):
    n = whole.shape[1]
    cut = [whole[:, :a]] if a else []
    cut.append(op(whole[:, a:b], part))
    if b < n:
        cut.append(whole[:, b:])
    return cut[0] if len(cut) == 1 else jnp.concatenate(cut, axis=1)


def combine_kernel(sizes, ways, copies, *refs):
    got = refs[:ways]
    info, margin = refs[ways:]
    tp = sizes[0]
    acc = jnp.zeros((1, 1), F32)
    for i in range(ways):
        parts = [got[j][(i - j) % ways] for j in range(ways)]
        peak = functools.reduce(jnp.maximum, [p[0:1] for p in parts])
        scales = [jnp.exp2(p[0:1] - peak) for p in parts]
        total = sum(s * p[1:2] for s, p in zip(scales, parts))
        delta = sum(s * p[2:3] for s, p in zip(scales, parts)) / total
        info[i, 0:1] = peak + jnp.log2(total)
        info[i, 1:2] = delta
        info[i, 2:3] = scales[0] / total
        acc = acc + jnp.sum(delta[:, HEADS * tp :], axis=1, keepdims=True)
    rest = sum(got[j][0, 3:4, 0:1] for j in range(ways)) / copies
    margin[...] = jnp.broadcast_to(BETA * (acc + rest), margin.shape)


def backward_kernel(sizes, slot, first, last, kv, qs, gs, ot, info, *refs):
    if first:
        odq, acc = refs
    elif last:
        *margins, before, odq, dkv = refs
    else:
        before, odq, acc = refs
    tp, tr, groups = sizes
    half = tp + 2 * tr
    n = 2 * tp + 4 * tr
    lanes = HEADS * half
    lim = [limits(p[0], slot) for p in pieces(sizes)]
    lse, delta, alpha = (info[slot, k : k + 1] for k in range(3))

    def put(blocks, off, rows, value):
        value = value.reshape(CHUNK // rows, rows, D)
        at = (blocks, slice(off, off + rows), slice(None))
        if not first:
            value = before[at] + value
        if last:
            dkv[at] = value.astype(BF16)
        else:
            acc[at] = value

    dq = jnp.zeros((D, lanes), F32)
    for step in steps(sizes):
        kind, chunk, a, b = step[:4]
        rows, _, _, koff, voff = pieces(sizes)[kind]
        blocks = slice(chunk * (CHUNK // rows), (chunk + 1) * (CHUNK // rows))
        p = jnp.exp2(scores(kv, qs, sizes, step, lim) * SCALE2 - lse[:, a:b])
        dp = mm(key_rows(kv, rows, voff, chunk), gs[a:b], NT)
        ds = (p * (dp - delta[:, a:b])).astype(BF16)
        put(blocks, voff, rows, mm(p.astype(BF16), gs[a:b], NN))
        put(blocks, koff, rows, mm(ds, qs[a:b], NN))
        dq = over(dq, mm(key_rows(kv, rows, koff, chunk), ds, TN), a, b, jnp.add)

    for base, whole in ((0, ot[...] * alpha), (half, dq)):
        turned = whole.T.astype(BF16)
        for rows, lane, row, _, _ in pieces(sizes):
            for h in range(HEADS):
                at = lane + h * rows
                odq[base + row : base + row + rows, h * D : (h + 1) * D] = turned[at : at + rows]
    if last:
        left = sum(m[...] for m in margins)
        row = lax.broadcasted_iota(jnp.int32, (16, D), 0)
        packed = jnp.zeros((16, D), F32)
        for i in range(3):
            part = left.astype(BF16).astype(F32)
            left = left - part
            packed = jnp.where(row == i, jnp.broadcast_to(part[0:1], (16, D)), packed)
        dkv[:, n : n + 16, :] = jnp.broadcast_to(packed.astype(BF16)[None], (groups, 16, D))


def outputs_kernel(sizes, mine, *refs):
    *others, p_out, r_out, dq = refs
    tp, tr, _ = sizes
    half = tp + 2 * tr

    def gathered(a, b):
        return mine[a:b].astype(F32) + sum(o[a:b].astype(F32) for o in others)

    p_out[...] = gathered(0, tp).astype(BF16)
    for s in range(2):
        r_out[s] = gathered(tp + s * tr, tp + (s + 1) * tr).astype(BF16)
    dq[...] = gathered(half, 2 * half)


def final_kernel(sizes, terms, dq, *refs):
    outs, (*held, sems) = refs[:5], refs[5:]
    p_dq, r_dq, p_dkv, r_dkv, loss = held
    tp, tr, groups = sizes
    n = 2 * tp + 4 * tr
    parts = jnp.sum(terms[:, n : n + 16, :].astype(F32), axis=0)
    margin = jnp.sum(parts[0:8], axis=0, keepdims=True)
    z = -margin
    loss[...] = jnp.maximum(z, 0.0) + jnp.log1p(jnp.exp(-jnp.abs(z)))
    weight = (-BETA / (1.0 + jnp.exp(margin)))[:, 0:1]
    copies = [pltpu.make_async_copy(a, b, sems.at[i]) for i, (a, b) in enumerate(zip(held, outs))]
    copies[4].start()
    scaled = weight * SCALE
    p_dq[...] = (dq[0:tp] * scaled).astype(BF16)
    copies[0].start()
    for s in range(2):
        a = tp + s * tr
        r_dq[s] = (dq[a : a + tr] * scaled).astype(BF16)
    copies[1].start()

    def summed(a, b, scale):
        return (jnp.sum(terms[:, a:b, :].astype(F32), axis=0) * scale).astype(BF16)

    for i, scale in enumerate((scaled, weight)):
        p_dkv[i] = summed(i * tp, (i + 1) * tp, scale)
        for s in range(2):
            a = 2 * tp + (2 * i + s) * tr
            r_dkv[i, s] = summed(a, a + tr, scale)
    copies[2].start()
    copies[3].start()
    for copy in copies:
        copy.wait()


VMEM = pl.BlockSpec(memory_space=pltpu.VMEM)
HBM = pl.BlockSpec(memory_space=pltpu.HBM)
sds = jax.ShapeDtypeStruct
held = pltpu.VMEM


def call(body, outs, ins, scratch=(), limit=32, aliases=None, flops=0):
    def run(*args):
        args = [
            pltpu.with_memory_space_constraint(x, pltpu.VMEM) if spec is VMEM else x
            for x, spec in zip(args, ins)
        ]
        return pl.pallas_call(
            body,
            out_shape=outs,
            in_specs=ins,
            out_specs=jax.tree.map(lambda _: VMEM, outs),
            scratch_shapes=list(scratch),
            input_output_aliases=aliases or {},
            cost_estimate=pl.CostEstimate(flops=flops, bytes_accessed=0, transcendentals=0),
            compiler_params=pltpu.CompilerParams(vmem_limit_bytes=limit * 1024 * 1024),
        )(*args)

    return run


def shift(x, axis, by):
    n = lax.axis_size(axis)
    return lax.ppermute(x, axis, [(i, (i + by) % n) for i in range(n)])


def per_device(pq, pkv, rq, rkv, labels, logp, probe, pprobe):
    tp, tr = pq.shape[0], rq.shape[1]
    groups, ways = lax.axis_size("prompt"), lax.axis_size("resp")
    copies = lax.axis_size("dp")
    sizes = (tp, tr, groups)
    wide = HEADS * D
    n = 2 * tp + 4 * tr
    half = tp + 2 * tr
    lanes = HEADS * half

    qg, kvb, rest = pl.pallas_call(
        functools.partial(pack_kernel, sizes),
        out_shape=(held((2 * half, wide), BF16), held((groups, n, D), BF16), held((8, D), F32)),
        in_specs=[HBM] * 8,
        out_specs=(VMEM, VMEM, VMEM),
        scratch_shapes=[
            pltpu.VMEM(pkv.shape, BF16),
            pltpu.VMEM(rkv.shape, BF16),
            pltpu.VMEM(labels.shape, jnp.int32),
            pltpu.VMEM(logp.shape, F32),
            pltpu.VMEM(probe.shape, BF16),
            pltpu.SemaphoreType.DMA((9,)),
        ],
        compiler_params=pltpu.CompilerParams(vmem_limit_bytes=16 * 1024 * 1024),
    )(*[
        pltpu.with_memory_space_constraint(x, pltpu.HBM)
        for x in (pq, pkv, rq, rkv, labels, logp, probe, pprobe)
    ])
    kv = lax.all_to_all(kvb, "prompt", 0, 0, tiled=True)
    order = [0, 1, ways - 1] + list(range(2, ways - 1))
    stats, kept = rest, {}
    for slot in order:
        block = shift(qg, "resp", slot) if slot else qg
        qs, gs, ot, stats = call(
            functools.partial(forward_kernel, sizes, slot),
            (
                held((lanes, D), BF16),
                held((lanes, D), BF16),
                held((D, lanes), F32),
                held((ways, 4, lanes), F32),
            ),
            [VMEM] * 3,
            [pltpu.VMEM((CHUNK * len(steps(sizes)), lanes), F32)],
            aliases={2: 3} if slot else None,
            flops=2 * 2 * groups * half * lanes * D,
        )(kv, block, stats)
        kept[slot] = (qs, gs, ot)
    info, margin = call(
        functools.partial(combine_kernel, sizes, ways, copies),
        (held((ways, 3, lanes), F32), held((8, D), F32)),
        [VMEM] * ways,
    )(stats, *[shift(stats, "resp", j) for j in range(1, ways)])
    margins = [margin] + [shift(margin, "dp", j) for j in range(1, copies)]

    order = order[1:] + [0]
    backs, acc = {}, None
    for slot in order:
        first, last = slot == order[0], slot == order[-1]
        extra = margins if last else []
        if not first:
            extra = extra + [acc]
        end = held((groups, n + 16, D), BF16) if last else held((groups, n, D), F32)
        odq, acc = call(
            functools.partial(backward_kernel, sizes, slot, first, last),
            (held((2 * half, wide), BF16), end),
            [VMEM] * (5 + len(extra)),
            aliases={5: 1} if not first and not last else None,
            flops=5 * 2 * groups * half * lanes * D,
        )(kv, *kept[slot], info, *extra)
        backs[slot] = shift(odq, "resp", -slot) if slot else odq
    terms = lax.all_to_all(acc, "prompt", 0, 0, tiled=True)

    p_out, r_out, dq = call(
        functools.partial(outputs_kernel, sizes),
        (sds(pq.shape, BF16), sds(rq.shape, BF16), held((half, wide), F32)),
        [VMEM] * ways,
    )(*[backs[j] for j in range(ways)])
    last_outs = [
        (pq.shape, BF16),
        (rq.shape, BF16),
        (pkv.shape, BF16),
        (rkv.shape, BF16),
        ((1, D), F32),
    ]
    p_dq, r_dq, p_dkv, r_dkv, loss = pl.pallas_call(
        functools.partial(final_kernel, sizes),
        out_shape=tuple(sds(*o) for o in last_outs),
        in_specs=[VMEM] * 2,
        out_specs=(HBM,) * 5,
        scratch_shapes=[pltpu.VMEM(*o) for o in last_outs] + [pltpu.SemaphoreType.DMA((5,))],
        compiler_params=pltpu.CompilerParams(vmem_limit_bytes=16 * 1024 * 1024),
    )(*[pltpu.with_memory_space_constraint(x, pltpu.VMEM) for x in (terms, dq)])
    return (p_out, r_out, p_dq, r_dq, p_dkv, r_dkv, loss[0, 0])


def solution(mesh):
    placed = (
        P(("prompt", "resp"), "dp"),
        P(None, ("prompt", "resp"), "dp"),
        P(None, ("prompt", "resp"), "dp"),
        P(None, None, ("prompt", "resp"), "dp"),
        P(None, ("prompt", "resp")),
        P(None, ("prompt", "resp")),
        P(None, ("prompt", "resp"), "dp"),
        P(("prompt", "resp"), "dp"),
    )
    return jax.shard_map(
        per_device,
        mesh=mesh,
        in_specs=placed,
        out_specs=(
            P(("prompt", "resp"), "dp"),
            P(None, ("prompt", "resp"), "dp"),
            P(("prompt", "resp"), "dp"),
            P(None, ("prompt", "resp"), "dp"),
            P(None, ("prompt", "resp"), "dp"),
            P(None, None, ("prompt", "resp"), "dp"),
            P(),
        ),
        check_vma=False,
    )
```

```python
import functools
import math

import jax
import jax.numpy as jnp
from jax import lax
from jax.experimental import pallas as pl
from jax.experimental.pallas import tpu as pltpu
from jax.sharding import PartitionSpec as P

QUERY_HEADS = 32
KEY_VALUE_HEADS = 4
HEAD_SIZE = 128
BETA = 0.1
HIDDEN = -1e30
FLOOR = -1e29
SCALE = HEAD_SIZE ** -0.5
SCALE2 = SCALE * math.log2(math.e)

HEADS = QUERY_HEADS // KEY_VALUE_HEADS
D = HEAD_SIZE
BF16 = jnp.bfloat16
F32 = jnp.float32
CLASSES = 4

NT = (((1,), (1,)), ((), ()))
TN = (((0,), (0,)), ((), ()))
NN = (((1,), (0,)), ((), ()))


def mm(a, b, dims):
    return lax.dot_general(a, b, dims, preferred_element_type=F32)


def counted_rows(labels):
    row = lax.broadcasted_iota(jnp.int32, labels.shape, 0)
    return labels.astype(F32) * jnp.where(row == 0, 1.0, -1.0)


def as_column(row):
    n = row.shape[1]
    r = lax.broadcasted_iota(jnp.int32, (n, n), 0)
    c = lax.broadcasted_iota(jnp.int32, (n, n), 1)
    return jnp.sum(jnp.where(r == c, jnp.broadcast_to(row, (n, n)), 0.0), axis=1, keepdims=True)


def pack_kernel(sizes, pq, pkv, rq, rkv, labels, logp, probe, pprobe, *refs):
    qg, block, rest, labels_in, logp_in, probe_in, sems = refs
    tp, tr, _ = sizes
    half = tp + 2 * tr
    moves = [
        (labels, labels_in),
        (probe, probe_in),
        (logp, logp_in),
        (pq, qg.at[0:tp]),
        (rq.at[0], qg.at[tp : tp + tr]),
        (rq.at[1], qg.at[tp + tr : half]),
        (pprobe, qg.at[half : half + tp]),
    ]
    for i in range(2):
        moves.append((pkv.at[i], block.at[i * tp : (i + 1) * tp]))
        for s in range(2):
            base = 2 * tp + (2 * i + s) * tr
            moves.append((rkv.at[i, s], block.at[base : base + tr]))
    copies = [pltpu.make_async_copy(a, b, sems.at[i]) for i, (a, b) in enumerate(moves)]
    for copy in copies:
        copy.start()
    copies[0].wait()
    copies[1].wait()
    counted = counted_rows(labels_in[...])
    for s in range(2):
        col = as_column(counted[s : s + 1])
        base = half + tp + s * tr
        qg[base : base + tr] = (probe_in[s].astype(F32) * col).astype(BF16)
    copies[2].wait()
    rest[...] = jnp.broadcast_to(
        jnp.sum(counted * logp_in[...], axis=(0, 1), keepdims=True), rest.shape
    )
    for copy in copies[3:]:
        copy.wait()


def join_kernel(block, *refs):
    *others, joined = refs
    others = others[: joined.shape[0] - 1]
    members = len(others) + 1
    mine = lax.axis_index("prompt") // CLASSES
    for k, ref in enumerate((block, *others)):
        joined[pl.ds(lax.rem(mine + members - k, members), 1)] = ref[...][None]


def limits(rows, slot, other):
    g, y = lax.axis_index("prompt"), lax.axis_index("resp")
    member, mine = g // CLASSES, lax.rem(g, CLASSES)
    if other:
        return (member + ((mine ^ other) < mine).astype(jnp.int32)) * rows
    if slot == 0:
        lane = lax.broadcasted_iota(jnp.int32, (1, HEADS * rows), 1)
        return member * rows + lane % rows + 1
    return member * rows + jnp.where(slot > y, rows, 0)


def hide(s, lim):
    key = lax.broadcasted_iota(jnp.int32, s.shape, 0)
    return jnp.where(key < lim, s, HIDDEN)


def pieces(sizes):
    tp, tr, _ = sizes
    out = [(tp, 0, 0, 0, tp)]
    for s in range(2):
        out.append((tr, HEADS * (tp + s * tr), tp + s * tr, 2 * tp + s * tr, 2 * tp + (2 + s) * tr))
    return out


def steps(sizes, prompt_groups, resp_groups):
    tp, tr, _ = sizes
    full = HEADS * (tp + 2 * tr)
    out = [(0, classes, 0, full, HEADS * tp) for classes in prompt_groups]
    for kind, (rows, lane, *_) in enumerate(pieces(sizes)):
        if kind:
            wide = HEADS * rows
            out += [(kind, classes, lane, lane + wide, wide) for classes in resp_groups]
    return out


def key_rows(kv, rows, base, classes):
    parts = [kv[e][:, base : base + rows, :].reshape(-1, D) for e in classes]
    return parts[0] if len(parts) == 1 else jnp.concatenate(parts, axis=0)


def scores(kv, q, sizes, step, slot):
    kind, classes, a, b, masked = step
    rows, _, _, koff, _ = pieces(sizes)[kind]
    s = mm(key_rows(kv, rows, koff, classes), q[a:b], NT)
    n = s.shape[0] // len(classes)
    parts = [
        hide(s[i * n : (i + 1) * n, :masked], limits(rows, slot, e)) for i, e in enumerate(classes)
    ]
    shown = parts[0] if len(parts) == 1 else jnp.concatenate(parts, axis=0)
    return shown if masked == b - a else jnp.concatenate([shown, s[:, masked:]], axis=1)


def over(whole, part, a, b, op):
    n = whole.shape[1]
    cut = [whole[:, :a]] if a else []
    cut.append(op(whole[:, a:b], part))
    if b < n:
        cut.append(whole[:, b:])
    return cut[0] if len(cut) == 1 else jnp.concatenate(cut, axis=1)


def eights(x):
    return x.reshape(-1, 8, x.shape[1])


def spread(sizes, whole, ref):
    turned = whole.T.astype(BF16)
    for rows, lane, row, _, _ in pieces(sizes):
        for h in range(HEADS):
            at = lane + h * rows
            ref[row : row + rows, h * D : (h + 1) * D] = turned[at : at + rows]


def forward_steps(sizes):
    return steps(sizes, [(0, 1), (2, 3)], [(0, 1, 2, 3)])


def forward_kernel(sizes, slot, *refs):
    kv, qg = refs[:CLASSES], refs[CLASSES]
    rest, qs, gs, part_out, stats, s_scr = refs[CLASSES + 1 :]
    if slot == 0:
        stats[...] = jnp.zeros(stats.shape, F32)
    tp, tr, groups = sizes
    half = tp + 2 * tr
    lanes = HEADS * half
    for rows, lane, row, _, _ in pieces(sizes):
        for h in range(HEADS):
            at = lane + h * rows
            qs[at : at + rows] = qg[row : row + rows, h * D : (h + 1) * D]
            gs[at : at + rows] = qg[half + row : half + row + rows, h * D : (h + 1) * D]

    peak = jnp.full((8, lanes), FLOOR, F32)
    spans, base = [], 0
    for step in forward_steps(sizes):
        a, b = step[2:4]
        s = scores(kv, qs, sizes, step, slot)
        spans.append((base, base + s.shape[0]))
        base += s.shape[0]
        s_scr[spans[-1][0] : base, a:b] = s
        peak = over(peak, jnp.max(eights(s), axis=0), a, b, jnp.maximum)
    peak = jnp.max(peak, axis=0, keepdims=True) * SCALE2

    total = jnp.zeros((8, lanes), F32)
    out = jnp.zeros((D, lanes), F32)
    for (lo, hi), (kind, classes, a, b, _) in zip(spans, forward_steps(sizes)):
        rows, _, _, _, voff = pieces(sizes)[kind]
        p = jnp.exp2(s_scr[lo:hi, a:b] * SCALE2 - peak[:, a:b])
        part = mm(key_rows(kv, rows, voff, classes), p.astype(BF16), TN)
        out = over(out, part, a, b, jnp.add)
        total = over(total, jnp.sum(eights(p), axis=0), a, b, jnp.add)
    total = jnp.sum(total, axis=0, keepdims=True)
    stats[slot, 0:1] = peak
    stats[slot, 1:2] = total
    stats[slot, 2:3] = jnp.sum(out * gs[...].astype(F32).T, axis=0, keepdims=True)
    if slot == 0:
        stats[slot, 3:4, 0:D] = rest[0:1]
    spread(sizes, out * (1.0 / jnp.maximum(total, 1e-30)), part_out)


def combine_kernel(sizes, ways, copies, *refs):
    got = refs[:ways]
    info, shares, margin = refs[ways:]
    tp = sizes[0]
    acc = jnp.zeros((1, 1), F32)
    shares[...] = jnp.zeros(shares.shape, F32)
    for i in range(ways):
        parts = [got[j][(i - j) % ways] for j in range(ways)]
        peak = functools.reduce(jnp.maximum, [p[0:1] for p in parts])
        scales = [jnp.exp2(p[0:1] - peak) for p in parts]
        total = sum(s * p[1:2] for s, p in zip(scales, parts))
        delta = sum(s * p[2:3] for s, p in zip(scales, parts)) / total
        info[i, 0:1] = peak + jnp.log2(total)
        info[i, 1:2] = delta
        acc = acc + jnp.sum(delta[:, HEADS * tp :], axis=1, keepdims=True)
        if i == 0:
            for k in range(ways):
                j = -k % ways
                shares[k : k + 1] = scales[j] * parts[j][1:2] / total
    rest = sum(got[j][0, 3:4, 0:1] for j in range(ways)) / copies
    margin[...] = jnp.broadcast_to(BETA * (acc + rest), margin.shape)


def stamp(value, ref, at):
    row = lax.broadcasted_iota(jnp.int32, (16, D), 0)
    packed = jnp.zeros((16, D), F32)
    for i in range(3):
        part = value.astype(BF16).astype(F32)
        value = value - part
        packed = jnp.where(row == i, jnp.broadcast_to(part[0:1], (16, D)), packed)
    ref[at : at + 16] = packed.astype(BF16)


def stamped(ref, at):
    return jnp.sum(ref[at : at + 8].astype(F32), axis=0, keepdims=True)


def stamp_kernel(ways, *refs):
    margins, ins, outs = refs[:ways], refs[ways:-2], refs[-2:]
    total = sum(m[...] for m in margins)
    for out in outs:
        stamp(total, out, out.shape[0] - 16)


def backward_kernel(sizes, classes, ways, copies, first, last, *refs):
    refs = list(refs)

    def take(n):
        got = refs[:n]
        del refs[:n]
        return got

    kv = dict(zip(classes, take(len(classes))))
    qs, gs = take(ways), take(ways)
    (info,) = take(1)
    if last:
        take(ways - 1)
    margins = take(copies) if copies else None
    before = None if first else take(1)[0]
    outs = take(len(classes))
    ends = take(ways if last else 1)
    (acc,) = refs
    tp, tr, groups = sizes
    members = groups // CLASSES
    lanes = HEADS * (tp + 2 * tr)
    todo = steps(sizes, [tuple(classes)], [tuple(classes)])

    for slot in range(ways):
        lse, delta = (info[slot, k : k + 1] for k in range(2))
        dq = jnp.zeros((D, lanes), F32) if first else before[slot]
        for step in todo:
            kind, _, a, b, _ = step
            rows, _, _, koff, voff = pieces(sizes)[kind]

            def put(off, value):
                value = value.reshape(len(classes), members, rows, D)
                at = (slice(None), slice(None), slice(off, off + rows), slice(None))
                acc[at] = value if slot == 0 else acc[at] + value

            p = jnp.exp2(scores(kv, qs[slot], sizes, step, slot) * SCALE2 - lse[:, a:b])
            dp = mm(key_rows(kv, rows, voff, classes), gs[slot][a:b], NT)
            ds = (p * (dp - delta[:, a:b])).astype(BF16)
            put(voff, mm(p.astype(BF16), gs[slot][a:b], NN))
            put(koff, mm(ds, qs[slot][a:b], NN))
            dq = over(dq, mm(key_rows(kv, rows, koff, classes), ds, TN), a, b, jnp.add)
        if last:
            spread(sizes, dq, ends[slot])
        else:
            ends[0][slot] = dq
    for i, out in enumerate(outs):
        terms = acc[i].reshape(-1, D)
        out[0 : terms.shape[0]] = terms.astype(out.dtype)
        if margins:
            stamp(sum(m[...] for m in margins), out, terms.shape[0])


def middle_kernel(sizes, copies, mine, *refs):
    got, refs = refs[: CLASSES - 1], refs[CLASSES - 1 :]
    margins, (*sends, kept, margin) = refs[:copies], refs[copies:]
    tp, tr, groups = sizes
    n, members = 2 * tp + 4 * tr, groups // CLASSES
    at = lax.axis_index("prompt") // CLASSES
    total = sum(m[0:1] for m in margins) + sum(stamped(r, members * n) for r in got)
    margin[...] = jnp.broadcast_to(total, margin.shape)

    def summed(k):
        block = pl.ds(pl.multiple_of(lax.rem(at + k, members) * n, n), n)
        return mine[block] + sum(r[block].astype(F32) for r in got)

    for k, send in enumerate(sends):
        send[0:n] = summed(k + 1).astype(BF16)
        stamp(jnp.broadcast_to(total, (8, D)), send, n)
    kept[...] = summed(0)


def outputs_kernel(sizes, shares, *refs):
    *blocks, p_out, r_out = refs
    cols = shares[...].T
    for kind, (rows, lane, row, _, _) in enumerate(pieces(sizes)):
        for h in range(HEADS):
            at = lane + h * rows
            value = sum(
                o[row : row + rows, h * D : (h + 1) * D].astype(F32) * cols[at : at + rows, i : i + 1]
                for i, o in enumerate(blocks)
            ).astype(BF16)
            if kind == 0:
                p_out[:, h * D : (h + 1) * D] = value
            else:
                r_out[kind - 1, :, h * D : (h + 1) * D] = value


def final_kernel(sizes, ways, *refs):
    dqs, refs = refs[:ways], refs[ways:]
    tp, tr, groups = sizes
    n, members = 2 * tp + 4 * tr, groups // CLASSES
    kept, margin_in, *got = refs[: 1 + members]
    refs = refs[1 + members :]
    outs, (*held, sems) = refs[:5], refs[5:]
    p_dq, r_dq, p_dkv, r_dkv, loss = held
    margin = margin_in[0:1] + sum(stamped(r, n) for r in got)
    z = -margin
    loss[...] = jnp.maximum(z, 0.0) + jnp.log1p(jnp.exp(-jnp.abs(z)))
    weight = (-BETA / (1.0 + jnp.exp(margin)))[:, 0:1]
    copies = [pltpu.make_async_copy(a, b, sems.at[i]) for i, (a, b) in enumerate(zip(held, outs))]
    copies[4].start()
    scaled = weight * SCALE

    def gathered(a, b):
        return (sum(r[a:b].astype(F32) for r in dqs) * scaled).astype(BF16)

    p_dq[...] = gathered(0, tp)
    copies[0].start()
    for s in range(2):
        r_dq[s] = gathered(tp + s * tr, tp + (s + 1) * tr)
    copies[1].start()

    def summed(a, b, scale):
        return ((kept[a:b] + sum(r[a:b].astype(F32) for r in got)) * scale).astype(BF16)

    for i, scale in enumerate((scaled, weight)):
        p_dkv[i] = summed(i * tp, (i + 1) * tp, scale)
        for s in range(2):
            a = 2 * tp + (2 * i + s) * tr
            r_dkv[i, s] = summed(a, a + tr, scale)
    copies[2].start()
    copies[3].start()
    for copy in copies:
        copy.wait()


VMEM = pl.BlockSpec(memory_space=pltpu.VMEM)
HBM = pl.BlockSpec(memory_space=pltpu.HBM)
sds = jax.ShapeDtypeStruct
held = pltpu.VMEM


def call(body, outs, ins, scratch=(), limit=32, aliases=None, flops=0, specs=None):
    def run(*args):
        args = [
            pltpu.with_memory_space_constraint(x, pltpu.VMEM if ins is VMEM else pltpu.HBM)
            for x in args
        ]
        return pl.pallas_call(
            body,
            out_shape=outs,
            in_specs=[ins] * len(args),
            out_specs=specs or jax.tree.map(lambda _: VMEM, outs),
            scratch_shapes=list(scratch),
            input_output_aliases=aliases or {},
            cost_estimate=pl.CostEstimate(flops=flops, bytes_accessed=0, transcendentals=0),
            compiler_params=pltpu.CompilerParams(vmem_limit_bytes=limit * 1024 * 1024),
        )(*args)

    return run


def shift(x, axis, by):
    n = lax.axis_size(axis)
    return lax.ppermute(x, axis, [(i, (i + by) % n) for i in range(n)])


def swap(x, other):
    return lax.ppermute(x, "prompt", [(i, i ^ other) for i in range(lax.axis_size("prompt"))])


def per_device(pq, pkv, rq, rkv, labels, logp, probe, pprobe):
    tp, tr = pq.shape[0], rq.shape[1]
    groups, ways = lax.axis_size("prompt"), lax.axis_size("resp")
    copies = lax.axis_size("dp")
    members = groups // CLASSES
    sizes = (tp, tr, groups)
    wide = HEADS * D
    n = 2 * tp + 4 * tr
    half = tp + 2 * tr
    lanes = HEADS * half

    qg, block, rest = call(
        functools.partial(pack_kernel, sizes),
        (held((2 * half, wide), BF16), held((n, D), BF16), held((8, D), F32)),
        HBM,
        [
            pltpu.VMEM(labels.shape, jnp.int32),
            pltpu.VMEM(logp.shape, F32),
            pltpu.VMEM(probe.shape, BF16),
            pltpu.SemaphoreType.DMA((13,)),
        ],
        limit=16,
    )(pq, pkv, rq, rkv, labels, logp, probe, pprobe)
    queries = [qg] + [shift(qg, "resp", j) for j in range(1, ways)]
    joined = call(join_kernel, held((members, n, D), BF16), VMEM, limit=16)(
        block, *[shift(block, "prompt", CLASSES * k) for k in range(1, members)],
        queries[1], queries[-1],
    )
    kv = [joined] + [swap(joined, e) for e in range(1, CLASSES)]

    order = [0, 1, ways - 1] + list(range(2, ways - 1))
    stats, kept = rest, {}
    scr = sum(len(c) * members * (tp if k == 0 else tr) for k, c, *_ in forward_steps(sizes))
    for slot in order:
        qs, gs, out, stats = call(
            functools.partial(forward_kernel, sizes, slot),
            (
                held((lanes, D), BF16),
                held((lanes, D), BF16),
                held((half, wide), BF16),
                held((ways, 4, lanes), F32),
            ),
            VMEM,
            [pltpu.VMEM((scr, lanes), F32)],
            aliases={CLASSES + 1: 3} if slot else None,
            flops=2 * 2 * groups * half * lanes * D,
        )(*kv, queries[slot], stats)
        kept[slot] = (qs, gs, out)
    qs, gs, outs = ([kept[j][i] for j in range(ways)] for i in range(3))
    all_stats = [stats, *[shift(stats, "resp", j) for j in range(1, ways)]]
    outs = [outs[0]] + [shift(outs[j], "resp", -j) for j in range(1, ways)]
    info, shares, margin = call(
        functools.partial(combine_kernel, sizes, ways, copies),
        (held((ways, 2, lanes), F32), held((8, lanes), F32), held((8, D), F32)),
        VMEM,
        limit=16,
    )(*all_stats)
    margins = [margin] + [shift(margin, "dp", j) for j in range(1, copies)]

    message = held((members * n + 16, D), BF16)
    plans = [(3, 1), (2,), (0,)]
    got, dq = {}, None
    for plan in plans:
        first, last = plan == plans[0], plan == plans[-1]
        extra = (margins if not first and not last else []) + ([] if first else [dq])
        if last:
            extra = outs[1:] + extra
        at = len(plan) + 2 * ways + 1 + len(extra) - 1
        results = call(
            functools.partial(
                backward_kernel, sizes, plan, ways, 0 if first or last else copies, first, last
            ),
            (held((members * n, D), F32), *[held((half, wide), BF16)] * ways)
            if last
            else (*[message] * len(plan), held((ways, D, lanes), F32)),
            VMEM,
            [pltpu.VMEM((len(plan), members, n, D), F32)],
            aliases=None if first or last else {at: len(plan)},
            flops=5 * 2 * members * len(plan) * half * lanes * D * ways,
        )(*[kv[e] for e in plan], *qs, *gs, info, *extra)
        if last:
            mine, *dqs = results
            continue
        *messages, dq = results
        if first:
            messages = call(
                functools.partial(stamp_kernel, copies),
                (message, message),
                VMEM,
                limit=16,
                aliases={copies: 0, copies + 1: 1},
            )(*margins, *messages)
        for e, m in zip(plan, messages):
            got[e] = swap(m, e)
    dqs = [dqs[0]] + [shift(dqs[j], "resp", -j) for j in range(1, ways)]
    *sends, part, margin = call(
        functools.partial(middle_kernel, sizes, copies),
        (*[held((n + 16, D), BF16)] * (members - 1), held((n, D), F32), held((8, D), F32)),
        VMEM,
        limit=16,
    )(mine, *[got[e] for e in range(1, CLASSES)], *margins)
    terms = [shift(x, "prompt", CLASSES * (k + 1)) for k, x in enumerate(sends)]

    p_out, r_out = call(
        functools.partial(outputs_kernel, sizes),
        (sds(pq.shape, BF16), sds(rq.shape, BF16)),
        VMEM,
        limit=16,
    )(shares, *outs)
    results = [
        (pq.shape, BF16),
        (rq.shape, BF16),
        (pkv.shape, BF16),
        (rkv.shape, BF16),
        ((1, D), F32),
    ]
    p_dq, r_dq, p_dkv, r_dkv, loss = call(
        functools.partial(final_kernel, sizes, ways),
        tuple(sds(*o) for o in results),
        VMEM,
        [pltpu.VMEM(*o) for o in results] + [pltpu.SemaphoreType.DMA((5,))],
        limit=16,
        specs=(HBM,) * 5,
    )(*dqs, part, margin, *terms)
    return (p_out, r_out, p_dq, r_dq, p_dkv, r_dkv, loss[0, 0])


def solution(mesh):
    placed = (
        P(("prompt", "resp"), "dp"),
        P(None, ("prompt", "resp"), "dp"),
        P(None, ("prompt", "resp"), "dp"),
        P(None, None, ("prompt", "resp"), "dp"),
        P(None, ("prompt", "resp")),
        P(None, ("prompt", "resp")),
        P(None, ("prompt", "resp"), "dp"),
        P(("prompt", "resp"), "dp"),
    )
    return jax.shard_map(
        per_device,
        mesh=mesh,
        in_specs=placed,
        out_specs=(
            P(("prompt", "resp"), "dp"),
            P(None, ("prompt", "resp"), "dp"),
            P(("prompt", "resp"), "dp"),
            P(None, ("prompt", "resp"), "dp"),
            P(None, ("prompt", "resp"), "dp"),
            P(None, None, ("prompt", "resp"), "dp"),
            P(),
        ),
        check_vma=False,
    )
```

```python
import functools
import math

import jax
import jax.numpy as jnp
from jax import lax
from jax.experimental import pallas as pl
from jax.experimental.pallas import tpu as pltpu
from jax.sharding import PartitionSpec as P

QUERY_HEADS = 32
KEY_VALUE_HEADS = 4
HEAD_SIZE = 128
BETA = 0.1
HIDDEN = -1e30
FLOOR = -1e29
SCALE = HEAD_SIZE ** -0.5
SCALE2 = SCALE * math.log2(math.e)

HEADS = QUERY_HEADS // KEY_VALUE_HEADS
D = HEAD_SIZE
BF16 = jnp.bfloat16
F32 = jnp.float32
CLASSES = 4

NT = (((1,), (1,)), ((), ()))
TN = (((0,), (0,)), ((), ()))
NN = (((1,), (0,)), ((), ()))


def mm(a, b, dims):
    return lax.dot_general(a, b, dims, preferred_element_type=F32)


def counted_rows(labels):
    row = lax.broadcasted_iota(jnp.int32, labels.shape, 0)
    return labels.astype(F32) * jnp.where(row == 0, 1.0, -1.0)


def as_column(row):
    n = row.shape[1]
    r = lax.broadcasted_iota(jnp.int32, (n, n), 0)
    c = lax.broadcasted_iota(jnp.int32, (n, n), 1)
    return jnp.sum(jnp.where(r == c, jnp.broadcast_to(row, (n, n)), 0.0), axis=1, keepdims=True)


def pack_kernel(sizes, pq, pkv, rq, rkv, labels, logp, probe, pprobe, *refs):
    qg, block, rest, labels_in, logp_in, probe_in, sems = refs
    tp, tr, _ = sizes
    half = tp + 2 * tr
    moves = [
        (labels, labels_in),
        (probe, probe_in),
        (logp, logp_in),
        (pq, qg.at[0:tp]),
        (rq.at[0], qg.at[tp : tp + tr]),
        (rq.at[1], qg.at[tp + tr : half]),
        (pprobe, qg.at[half : half + tp]),
    ]
    for i in range(2):
        moves.append((pkv.at[i], block.at[i * tp : (i + 1) * tp]))
        for s in range(2):
            base = 2 * tp + (2 * i + s) * tr
            moves.append((rkv.at[i, s], block.at[base : base + tr]))
    copies = [pltpu.make_async_copy(a, b, sems.at[i]) for i, (a, b) in enumerate(moves)]
    for copy in copies:
        copy.start()
    copies[0].wait()
    copies[1].wait()
    counted = counted_rows(labels_in[...])
    for s in range(2):
        col = as_column(counted[s : s + 1])
        base = half + tp + s * tr
        qg[base : base + tr] = (probe_in[s].astype(F32) * col).astype(BF16)
    copies[2].wait()
    rest[...] = jnp.broadcast_to(
        jnp.sum(counted * logp_in[...], axis=(0, 1), keepdims=True), rest.shape
    )
    for copy in copies[3:]:
        copy.wait()


def join_kernel(block, *refs):
    *others, joined = refs
    others = others[: joined.shape[0] - 1]
    members = len(others) + 1
    mine = lax.axis_index("prompt") // CLASSES
    for k, ref in enumerate((block, *others)):
        joined[pl.ds(lax.rem(mine + members - k, members), 1)] = ref[...][None]


def limits(rows, slot, other):
    g, y = lax.axis_index("prompt"), lax.axis_index("resp")
    member, mine = g // CLASSES, lax.rem(g, CLASSES)
    if other:
        return (member + ((mine ^ other) < mine).astype(jnp.int32)) * rows
    if slot == 0:
        lane = lax.broadcasted_iota(jnp.int32, (1, HEADS * rows), 1)
        return member * rows + lane % rows + 1
    return member * rows + jnp.where(slot > y, rows, 0)


def hide(s, lim):
    key = lax.broadcasted_iota(jnp.int32, s.shape, 0)
    return jnp.where(key < lim, s, HIDDEN)


def pieces(sizes):
    tp, tr, _ = sizes
    out = [(tp, 0, 0, 0, tp)]
    for s in range(2):
        out.append((tr, HEADS * (tp + s * tr), tp + s * tr, 2 * tp + s * tr, 2 * tp + (2 + s) * tr))
    return out


def steps(sizes, prompt_groups, resp_groups):
    tp, tr, _ = sizes
    full = HEADS * (tp + 2 * tr)
    out = [(0, classes, 0, full, HEADS * tp) for classes in prompt_groups]
    for kind, (rows, lane, *_) in enumerate(pieces(sizes)):
        if kind:
            wide = HEADS * rows
            out += [(kind, classes, lane, lane + wide, wide) for classes in resp_groups]
    return out


def key_rows(kv, rows, base, classes):
    parts = [kv[e][:, base : base + rows, :].reshape(-1, D) for e in classes]
    return parts[0] if len(parts) == 1 else jnp.concatenate(parts, axis=0)


def scores(kv, q, sizes, step, slot):
    kind, classes, a, b, masked = step
    rows, _, _, koff, _ = pieces(sizes)[kind]
    s = mm(key_rows(kv, rows, koff, classes), q[a:b], NT)
    n = s.shape[0] // len(classes)
    parts = [
        hide(s[i * n : (i + 1) * n, :masked], limits(rows, slot, e)) for i, e in enumerate(classes)
    ]
    shown = parts[0] if len(parts) == 1 else jnp.concatenate(parts, axis=0)
    return shown if masked == b - a else jnp.concatenate([shown, s[:, masked:]], axis=1)


def over(whole, part, a, b, op):
    n = whole.shape[1]
    cut = [whole[:, :a]] if a else []
    cut.append(op(whole[:, a:b], part))
    if b < n:
        cut.append(whole[:, b:])
    return cut[0] if len(cut) == 1 else jnp.concatenate(cut, axis=1)


def eights(x):
    return x.reshape(-1, 8, x.shape[1])


def spread(sizes, whole, ref):
    turned = whole.T.astype(BF16)
    for rows, lane, row, _, _ in pieces(sizes):
        for h in range(HEADS):
            at = lane + h * rows
            ref[row : row + rows, h * D : (h + 1) * D] = turned[at : at + rows]


def forward_steps(sizes):
    return steps(sizes, [(0, 1), (2, 3)], [(0, 1, 2, 3)])


def forward_kernel(sizes, slot, *refs):
    kv, qg = refs[:CLASSES], refs[CLASSES]
    rest, qs, gs, part_out, p_prompt, p_resp, stats, s_scr = refs[CLASSES + 1 :]
    if slot == 0:
        stats[...] = jnp.zeros(stats.shape, F32)
    tp, tr, groups = sizes
    half = tp + 2 * tr
    lanes = HEADS * half
    for rows, lane, row, _, _ in pieces(sizes):
        for h in range(HEADS):
            at = lane + h * rows
            qs[at : at + rows] = qg[row : row + rows, h * D : (h + 1) * D]
            gs[at : at + rows] = qg[half + row : half + row + rows, h * D : (h + 1) * D]

    peak = jnp.full((8, lanes), FLOOR, F32)
    spans, base = [], 0
    for step in forward_steps(sizes):
        a, b = step[2:4]
        s = scores(kv, qs, sizes, step, slot)
        spans.append((base, base + s.shape[0]))
        base += s.shape[0]
        s_scr[spans[-1][0] : base, a:b] = s
        peak = over(peak, jnp.max(eights(s), axis=0), a, b, jnp.maximum)
    peak = jnp.max(peak, axis=0, keepdims=True) * SCALE2

    total = jnp.zeros((8, lanes), F32)
    out = jnp.zeros((D, lanes), F32)
    for (lo, hi), (kind, classes, a, b, _) in zip(spans, forward_steps(sizes)):
        rows, _, _, _, voff = pieces(sizes)[kind]
        p = jnp.exp2(s_scr[lo:hi, a:b] * SCALE2 - peak[:, a:b])
        kept = p.astype(BF16)
        if kind == 0:
            at = classes[0] * (hi - lo) // len(classes)
            p_prompt[at : at + hi - lo] = kept
        else:
            p_resp[:, (kind - 1) * (b - a) : kind * (b - a)] = kept
        part = mm(key_rows(kv, rows, voff, classes), kept, TN)
        out = over(out, part, a, b, jnp.add)
        total = over(total, jnp.sum(eights(p), axis=0), a, b, jnp.add)
    total = jnp.sum(total, axis=0, keepdims=True)
    stats[slot, 0:1] = peak
    stats[slot, 1:2] = total
    stats[slot, 2:3] = jnp.sum(out * gs[...].astype(F32).T, axis=0, keepdims=True)
    if slot == 0:
        stats[slot, 3:4, 0:D] = rest[0:1]
    spread(sizes, out * (1.0 / jnp.maximum(total, 1e-30)), part_out)


def combine_kernel(sizes, ways, copies, *refs):
    got, gs = refs[:ways], refs[ways : 2 * ways]
    info, shares, margin, scaled = refs[2 * ways :]
    tp = sizes[0]
    acc = jnp.zeros((1, 1), F32)
    shares[...] = jnp.zeros(shares.shape, F32)
    factors = []
    for i in range(ways):
        parts = [got[j][(i - j) % ways] for j in range(ways)]
        peak = functools.reduce(jnp.maximum, [p[0:1] for p in parts])
        scales = [jnp.exp2(p[0:1] - peak) for p in parts]
        total = sum(s * p[1:2] for s, p in zip(scales, parts))
        delta = sum(s * p[2:3] for s, p in zip(scales, parts)) / total
        factor = scales[0] / total
        factors.append(factor)
        info[i : i + 1] = delta * factor
        acc = acc + jnp.sum(delta[:, HEADS * tp :], axis=1, keepdims=True)
        if i == 0:
            for k in range(ways):
                j = -k % ways
                shares[k : k + 1] = scales[j] * parts[j][1:2] / total
    rest = sum(got[j][0, 3:4, 0:1] for j in range(ways)) / copies
    margin[...] = jnp.broadcast_to(BETA * (acc + rest), margin.shape)
    while len(factors) < 8:
        factors.append(jnp.zeros_like(factors[0]))
    cols = jnp.concatenate(factors, axis=0).T
    for i in range(ways):
        scaled[i] = (gs[i][...].astype(F32) * cols[:, i : i + 1]).astype(BF16)


def stamp(value, ref, at):
    row = lax.broadcasted_iota(jnp.int32, (16, D), 0)
    packed = jnp.zeros((16, D), F32)
    for i in range(3):
        part = value.astype(BF16).astype(F32)
        value = value - part
        packed = jnp.where(row == i, jnp.broadcast_to(part[0:1], (16, D)), packed)
    ref[at : at + 16] = packed.astype(BF16)


def stamped(ref, at):
    return jnp.sum(ref[at : at + 8].astype(F32), axis=0, keepdims=True)


def stamp_kernel(ways, *refs):
    margins, ins, outs = refs[:ways], refs[ways:-2], refs[-2:]
    total = sum(m[...] for m in margins)
    for out in outs:
        stamp(total, out, out.shape[0] - 16)


def backward_kernel(sizes, classes, ways, copies, *refs):
    refs = list(refs)

    def take(n):
        got = refs[:n]
        del refs[:n]
        return got

    kv = dict(zip(classes, take(len(classes))))
    qs = take(ways)
    take(2 * ways)
    gs, info = take(2)
    margins = take(copies) if copies else None
    *outs, acc = refs[-1 - len(classes) - 2 * ways :]
    outs, p_prompt, p_resp = outs[: -2 * ways], outs[-2 * ways : -ways], outs[-ways:]
    tp, tr, groups = sizes
    members = groups // CLASSES

    for slot in range(ways):
        for kind, _, a, b, _ in steps(sizes, [tuple(classes)], [tuple(classes)]):
            rows, _, _, koff, voff = pieces(sizes)[kind]
            keys = members * rows

            def put(off, value):
                value = value.reshape(len(classes), members, rows, D)
                at = (slice(None), slice(None), slice(off, off + rows), slice(None))
                acc[at] = value if slot == 0 else acc[at] + value

            ref = p_resp[slot] if kind else p_prompt[slot]
            side = slice((kind - 1) * (b - a), kind * (b - a)) if kind else slice(None)
            spans = [slice(e * keys, (e + 1) * keys) for e in classes]
            parts = [ref[span, side] for span in spans]
            p = parts[0] if len(parts) == 1 else jnp.concatenate(parts, axis=0)
            grad = gs[slot, a:b]
            dp = mm(key_rows(kv, rows, voff, classes), grad, NT)
            put(voff, mm(p, grad, NN))
            ds = (p.astype(F32) * (dp - info[slot : slot + 1, a:b])).astype(BF16)
            put(koff, mm(ds, qs[slot][a:b], NN))
            for i, span in enumerate(spans):
                ref[span, side] = ds[i * keys : (i + 1) * keys]
    for i, out in enumerate(outs):
        terms = acc[i].reshape(-1, D)
        out[0 : terms.shape[0]] = terms.astype(out.dtype)
        if margins:
            stamp(sum(m[...] for m in margins), out, terms.shape[0])


def queries_kernel(sizes, slots, *refs):
    kv, refs = refs[:CLASSES], refs[CLASSES:]
    n = len(slots)
    lanes = HEADS * (sizes[0] + 2 * sizes[1])
    for ds_prompt, ds_resp, end in zip(refs[:n], refs[n : 2 * n], refs[2 * n :]):
        dq = jnp.zeros((D, lanes), F32)
        for kind, classes, a, b, _ in forward_steps(sizes):
            rows, _, _, koff, _ = pieces(sizes)[kind]
            keys = sizes[2] // CLASSES * rows
            span = slice(classes[0] * keys, (classes[-1] + 1) * keys)
            side = slice((kind - 1) * (b - a), kind * (b - a)) if kind else slice(None)
            ds = (ds_resp if kind else ds_prompt)[span, side]
            dq = over(dq, mm(key_rows(kv, rows, koff, classes), ds, TN), a, b, jnp.add)
        spread(sizes, dq, end)


def middle_kernel(sizes, copies, shifts, mine, *refs):
    got, refs = refs[: CLASSES - 1], refs[CLASSES - 1 :]
    margins, outs = refs[:copies], refs[-len(shifts) :]
    tp, tr, groups = sizes
    n, members = 2 * tp + 4 * tr, groups // CLASSES
    at = lax.axis_index("prompt") // CLASSES
    total = sum(m[0:1] for m in margins) + sum(stamped(r, members * n) for r in got)
    for k, out in zip(shifts, outs):
        block = pl.ds(pl.multiple_of(lax.rem(at + k, members) * n, n), n)
        terms = mine[block] + sum(r[block].astype(F32) for r in got)
        out[0:n] = terms.astype(out.dtype)
        if k:
            stamp(jnp.broadcast_to(total, (8, D)), out, n)
        else:
            out[n : n + 8] = jnp.broadcast_to(total, (8, D))


def outputs_kernel(sizes, shares, *refs):
    *blocks, p_out, r_out = refs
    cols = shares[...].T
    for kind, (rows, lane, row, _, _) in enumerate(pieces(sizes)):
        for h in range(HEADS):
            at = lane + h * rows
            value = sum(
                o[row : row + rows, h * D : (h + 1) * D].astype(F32) * cols[at : at + rows, i : i + 1]
                for i, o in enumerate(blocks)
            ).astype(BF16)
            if kind == 0:
                p_out[:, h * D : (h + 1) * D] = value
            else:
                r_out[kind - 1, :, h * D : (h + 1) * D] = value


def final_kernel(sizes, ways, *refs):
    dqs, refs = refs[:ways], refs[ways:]
    tp, tr, groups = sizes
    n, members = 2 * tp + 4 * tr, groups // CLASSES
    *got, kept = refs[:members]
    refs = refs[members:]
    outs, (*held, sems) = refs[:5], refs[5:]
    p_dq, r_dq, p_dkv, r_dkv, loss = held
    margin = kept[n : n + 1] + sum(stamped(r, n) for r in got)
    z = -margin
    loss[...] = jnp.maximum(z, 0.0) + jnp.log1p(jnp.exp(-jnp.abs(z)))
    weight = (-BETA / (1.0 + jnp.exp(margin)))[:, 0:1]
    copies = [pltpu.make_async_copy(a, b, sems.at[i]) for i, (a, b) in enumerate(zip(held, outs))]
    copies[4].start()
    scaled = weight * SCALE

    def gathered(a, b):
        return (sum(r[a:b].astype(F32) for r in dqs) * scaled).astype(BF16)

    p_dq[...] = gathered(0, tp)
    copies[0].start()
    for s in range(2):
        r_dq[s] = gathered(tp + s * tr, tp + (s + 1) * tr)
    copies[1].start()

    def summed(a, b, scale):
        return ((kept[a:b] + sum(r[a:b].astype(F32) for r in got)) * scale).astype(BF16)

    for i, scale in enumerate((scaled, weight)):
        p_dkv[i] = summed(i * tp, (i + 1) * tp, scale)
        for s in range(2):
            a = 2 * tp + (2 * i + s) * tr
            r_dkv[i, s] = summed(a, a + tr, scale)
    copies[2].start()
    copies[3].start()
    for copy in copies:
        copy.wait()


VMEM = pl.BlockSpec(memory_space=pltpu.VMEM)
HBM = pl.BlockSpec(memory_space=pltpu.HBM)
sds = jax.ShapeDtypeStruct
held = pltpu.VMEM


def call(body, outs, ins, scratch=(), limit=32, aliases=None, flops=0, specs=None):
    def run(*args):
        args = [
            pltpu.with_memory_space_constraint(x, pltpu.VMEM if ins is VMEM else pltpu.HBM)
            for x in args
        ]
        return pl.pallas_call(
            body,
            out_shape=outs,
            in_specs=[ins] * len(args),
            out_specs=specs or jax.tree.map(lambda _: VMEM, outs),
            scratch_shapes=list(scratch),
            input_output_aliases=aliases or {},
            cost_estimate=pl.CostEstimate(flops=flops, bytes_accessed=0, transcendentals=0),
            compiler_params=pltpu.CompilerParams(vmem_limit_bytes=limit * 1024 * 1024),
        )(*args)

    return run


def shift(x, axis, by):
    n = lax.axis_size(axis)
    return lax.ppermute(x, axis, [(i, (i + by) % n) for i in range(n)])


def swap(x, other):
    return lax.ppermute(x, "prompt", [(i, i ^ other) for i in range(lax.axis_size("prompt"))])


def per_device(pq, pkv, rq, rkv, labels, logp, probe, pprobe):
    tp, tr = pq.shape[0], rq.shape[1]
    groups, ways = lax.axis_size("prompt"), lax.axis_size("resp")
    copies = lax.axis_size("dp")
    members = groups // CLASSES
    sizes = (tp, tr, groups)
    wide = HEADS * D
    n = 2 * tp + 4 * tr
    half = tp + 2 * tr
    lanes = HEADS * half

    qg, block, rest = call(
        functools.partial(pack_kernel, sizes),
        (held((2 * half, wide), BF16), held((n, D), BF16), held((8, D), F32)),
        HBM,
        [
            pltpu.VMEM(labels.shape, jnp.int32),
            pltpu.VMEM(logp.shape, F32),
            pltpu.VMEM(probe.shape, BF16),
            pltpu.SemaphoreType.DMA((13,)),
        ],
        limit=16,
    )(pq, pkv, rq, rkv, labels, logp, probe, pprobe)
    queries = [qg] + [shift(qg, "resp", j) for j in range(1, ways)]
    joined = call(join_kernel, held((members, n, D), BF16), VMEM, limit=16)(
        block, *[shift(block, "prompt", CLASSES * k) for k in range(1, members)],
        queries[1], queries[-1],
    )
    kv = [joined] + [swap(joined, e) for e in range(1, CLASSES)]

    order = [0, 1, ways - 1] + list(range(2, ways - 1))
    stats, kept = rest, {}
    scr = sum(len(c) * members * (tp if k == 0 else tr) for k, c, *_ in forward_steps(sizes))
    for slot in order:
        *made, stats = call(
            functools.partial(forward_kernel, sizes, slot),
            (
                held((lanes, D), BF16),
                held((lanes, D), BF16),
                held((half, wide), BF16),
                held((groups * tp, lanes), BF16),
                held((groups * tr, 2 * HEADS * tr), BF16),
                held((ways, 4, lanes), F32),
            ),
            VMEM,
            [pltpu.VMEM((scr, lanes), F32)],
            aliases={CLASSES + 1: 5} if slot else None,
            flops=2 * 2 * groups * half * lanes * D,
        )(*kv, queries[slot], stats)
        kept[slot] = made
    qs, gs, outs, p_prompt, p_resp = ([kept[j][i] for j in range(ways)] for i in range(5))
    all_stats = [stats, *[shift(stats, "resp", j) for j in range(1, ways)]]
    outs = [outs[0]] + [shift(outs[j], "resp", -j) for j in range(1, ways)]
    info, shares, margin, scaled = call(
        functools.partial(combine_kernel, sizes, ways, copies),
        (
            held((ways, lanes), F32),
            held((8, lanes), F32),
            held((8, D), F32),
            held((ways, lanes, D), BF16),
        ),
        VMEM,
        limit=16,
    )(*all_stats, *gs)
    margins = [margin] + [shift(margin, "dp", j) for j in range(1, copies)]

    message = held((members * n + 16, D), BF16)
    got = {}
    plans = [(3, 1), (2,), (0,)]
    for step, plan in enumerate(plans):
        first, last = step == 0, step == len(plans) - 1
        extra = margins if not first and not last else []
        ties = outs[1:] if last else []
        at = len(plan) + ways
        results = call(
            functools.partial(backward_kernel, sizes, plan, ways, len(extra)),
            (
                *([held((members * n, D), F32)] if last else [message] * len(plan)),
                *[held((groups * tp, lanes), BF16)] * ways,
                *[held((groups * tr, 2 * HEADS * tr), BF16)] * ways,
            ),
            VMEM,
            [pltpu.VMEM((len(plan), members, n, D), F32)],
            aliases={at + i: len(plan) + i for i in range(2 * ways)},
            flops=4 * 2 * members * len(plan) * half * lanes * D * ways,
        )(*[kv[e] for e in plan], *qs, *p_prompt, *p_resp, scaled, info, *extra, *ties)
        messages, p_prompt, p_resp = results[: len(plan)], results[len(plan) : -ways], results[-ways:]
        if first:
            messages = call(
                functools.partial(stamp_kernel, copies),
                (message, message),
                VMEM,
                limit=16,
                aliases={copies: 0, copies + 1: 1},
            )(*margins, *messages)
        for e, m in zip(plan, messages):
            got[e] = m if last else swap(m, e)
    mine, dqs = got[0], {}
    for slots in ((ways // 2, 1), tuple(j for j in range(ways) if j not in (ways // 2, 1))):
        made = call(
            functools.partial(queries_kernel, sizes, slots),
            (held((half, wide), BF16),) * len(slots),
            VMEM,
            flops=2 * groups * half * lanes * D * len(slots),
        )(*kv, *[p_prompt[j] for j in slots], *[p_resp[j] for j in slots])
        dqs.update(zip(slots, made))
    dqs = [dqs[0]] + [shift(dqs[j], "resp", -j) for j in range(1, ways)]
    terms = []
    for shifts, ties in (((members // 2, 1), []), ((members - 1, 0), [dqs[ways // 2]])):
        sends = call(
            functools.partial(middle_kernel, sizes, copies, shifts),
            tuple(held((n + 16, D), BF16) if k else held((n + 8, D), F32) for k in shifts),
            VMEM,
            limit=16,
        )(mine, *[got[e] for e in range(1, CLASSES)], *margins, *ties)
        for k, x in zip(shifts, sends):
            terms.append(shift(x, "prompt", CLASSES * k) if k else x)

    p_out, r_out = call(
        functools.partial(outputs_kernel, sizes),
        (sds(pq.shape, BF16), sds(rq.shape, BF16)),
        VMEM,
        limit=16,
    )(shares, *outs)
    results = [
        (pq.shape, BF16),
        (rq.shape, BF16),
        (pkv.shape, BF16),
        (rkv.shape, BF16),
        ((1, D), F32),
    ]
    p_dq, r_dq, p_dkv, r_dkv, loss = call(
        functools.partial(final_kernel, sizes, ways),
        tuple(sds(*o) for o in results),
        VMEM,
        [pltpu.VMEM(*o) for o in results] + [pltpu.SemaphoreType.DMA((5,))],
        limit=16,
        specs=(HBM,) * 5,
    )(*dqs, *terms)
    return (p_out, r_out, p_dq, r_dq, p_dkv, r_dkv, loss[0, 0])


def solution(mesh):
    placed = (
        P(("prompt", "resp"), "dp"),
        P(None, ("prompt", "resp"), "dp"),
        P(None, ("prompt", "resp"), "dp"),
        P(None, None, ("prompt", "resp"), "dp"),
        P(None, ("prompt", "resp")),
        P(None, ("prompt", "resp")),
        P(None, ("prompt", "resp"), "dp"),
        P(("prompt", "resp"), "dp"),
    )
    return jax.shard_map(
        per_device,
        mesh=mesh,
        in_specs=placed,
        out_specs=(
            P(("prompt", "resp"), "dp"),
            P(None, ("prompt", "resp"), "dp"),
            P(("prompt", "resp"), "dp"),
            P(None, ("prompt", "resp"), "dp"),
            P(None, ("prompt", "resp"), "dp"),
            P(None, None, ("prompt", "resp"), "dp"),
            P(),
        ),
        check_vma=False,
    )
```

```python
import functools
import math

import jax
import jax.numpy as jnp
from jax import lax
from jax.experimental import pallas as pl
from jax.experimental.pallas import tpu as pltpu
from jax.sharding import PartitionSpec as P

QUERY_HEADS = 32
KEY_VALUE_HEADS = 4
HEAD_SIZE = 128
BETA = 0.1
HIDDEN = -1e30
FLOOR = -1e29
SCALE = HEAD_SIZE ** -0.5
SCALE2 = SCALE * math.log2(math.e)

HEADS = QUERY_HEADS // KEY_VALUE_HEADS
D = HEAD_SIZE
BF16 = jnp.bfloat16
F32 = jnp.float32
CLASSES = 4

NT = (((1,), (1,)), ((), ()))
TN = (((0,), (0,)), ((), ()))
NN = (((1,), (0,)), ((), ()))


def mm(a, b, dims):
    return lax.dot_general(a, b, dims, preferred_element_type=F32)


def counted_rows(labels):
    row = lax.broadcasted_iota(jnp.int32, labels.shape, 0)
    return labels.astype(F32) * jnp.where(row == 0, 1.0, -1.0)


def as_column(row):
    n = row.shape[1]
    r = lax.broadcasted_iota(jnp.int32, (n, n), 0)
    c = lax.broadcasted_iota(jnp.int32, (n, n), 1)
    return jnp.sum(jnp.where(r == c, jnp.broadcast_to(row, (n, n)), 0.0), axis=1, keepdims=True)


def pack_kernel(sizes, pq, pkv, rq, rkv, labels, logp, probe, pprobe, *refs):
    qg, block, rest, labels_in, logp_in, probe_in, sems = refs
    tp, tr, _ = sizes
    half = tp + 2 * tr
    moves = [
        (labels, labels_in),
        (probe, probe_in),
        (logp, logp_in),
        (pq, qg.at[0:tp]),
        (rq.at[0], qg.at[tp : tp + tr]),
        (rq.at[1], qg.at[tp + tr : half]),
        (pprobe, qg.at[half : half + tp]),
    ]
    for i in range(2):
        moves.append((pkv.at[i], block.at[i * tp : (i + 1) * tp]))
        for s in range(2):
            base = 2 * tp + (2 * i + s) * tr
            moves.append((rkv.at[i, s], block.at[base : base + tr]))
    copies = [pltpu.make_async_copy(a, b, sems.at[i]) for i, (a, b) in enumerate(moves)]
    for copy in copies:
        copy.start()
    copies[0].wait()
    copies[1].wait()
    counted = counted_rows(labels_in[...])
    for s in range(2):
        col = as_column(counted[s : s + 1])
        base = half + tp + s * tr
        qg[base : base + tr] = (probe_in[s].astype(F32) * col).astype(BF16)
    copies[2].wait()
    rest[...] = jnp.broadcast_to(
        jnp.sum(counted * logp_in[...], axis=(0, 1), keepdims=True), rest.shape
    )
    for copy in copies[3:]:
        copy.wait()


def join_kernel(block, *refs):
    *others, joined = refs
    others = others[: joined.shape[0] - 1]
    members = len(others) + 1
    mine = lax.axis_index("prompt") // CLASSES
    for k, ref in enumerate((block, *others)):
        joined[pl.ds(lax.rem(mine + members - k, members), 1)] = ref[...][None]


def limits(rows, slot, other):
    g, y = lax.axis_index("prompt"), lax.axis_index("resp")
    member, mine = g // CLASSES, lax.rem(g, CLASSES)
    if other:
        return (member + ((mine ^ other) < mine).astype(jnp.int32)) * rows
    if slot == 0:
        lane = lax.broadcasted_iota(jnp.int32, (1, HEADS * rows), 1)
        return member * rows + lane % rows + 1
    return member * rows + jnp.where(slot > y, rows, 0)


def hide(s, lim):
    key = lax.broadcasted_iota(jnp.int32, s.shape, 0)
    return jnp.where(key < lim, s, HIDDEN)


def pieces(sizes):
    tp, tr, _ = sizes
    out = [(tp, 0, 0, 0, tp)]
    for s in range(2):
        out.append((tr, HEADS * (tp + s * tr), tp + s * tr, 2 * tp + s * tr, 2 * tp + (2 + s) * tr))
    return out


def steps(sizes, prompt_groups, resp_groups):
    tp, tr, _ = sizes
    full = HEADS * (tp + 2 * tr)
    out = [(0, classes, 0, full, HEADS * tp) for classes in prompt_groups]
    for kind, (rows, lane, *_) in enumerate(pieces(sizes)):
        if kind:
            wide = HEADS * rows
            out += [(kind, classes, lane, lane + wide, wide) for classes in resp_groups]
    return out


def key_rows(kv, rows, base, classes):
    parts = [kv[e][:, base : base + rows, :].reshape(-1, D) for e in classes]
    return parts[0] if len(parts) == 1 else jnp.concatenate(parts, axis=0)


def scores(kv, q, sizes, step, slot):
    kind, classes, a, b, masked = step
    rows, _, _, koff, _ = pieces(sizes)[kind]
    s = mm(key_rows(kv, rows, koff, classes), q[a:b], NT)
    n = s.shape[0] // len(classes)
    parts = [
        hide(s[i * n : (i + 1) * n, :masked], limits(rows, slot, e)) for i, e in enumerate(classes)
    ]
    shown = parts[0] if len(parts) == 1 else jnp.concatenate(parts, axis=0)
    return shown if masked == b - a else jnp.concatenate([shown, s[:, masked:]], axis=1)


def over(whole, part, a, b, op):
    n = whole.shape[1]
    cut = [whole[:, :a]] if a else []
    cut.append(op(whole[:, a:b], part))
    if b < n:
        cut.append(whole[:, b:])
    return cut[0] if len(cut) == 1 else jnp.concatenate(cut, axis=1)


def eights(x):
    return x.reshape(-1, 8, x.shape[1])


def spread(sizes, whole, ref):
    turned = whole.T.astype(BF16)
    for rows, lane, row, _, _ in pieces(sizes):
        for h in range(HEADS):
            at = lane + h * rows
            ref[row : row + rows, h * D : (h + 1) * D] = turned[at : at + rows]


def forward_steps(sizes):
    return steps(sizes, [(0, 1), (2, 3)], [(0, 1, 2, 3)])


def forward_kernel(sizes, slot, *refs):
    kv, qg = refs[:CLASSES], refs[CLASSES]
    rest, qs, gs, part_out, p_prompt, p_resp, stats, s_scr = refs[CLASSES + 1 :]
    if slot == 0:
        stats[...] = jnp.zeros(stats.shape, F32)
    tp, tr, groups = sizes
    half = tp + 2 * tr
    lanes = HEADS * half
    for rows, lane, row, _, _ in pieces(sizes):
        for h in range(HEADS):
            at = lane + h * rows
            qs[at : at + rows] = qg[row : row + rows, h * D : (h + 1) * D]
            gs[at : at + rows] = qg[half + row : half + row + rows, h * D : (h + 1) * D]

    peak = jnp.full((8, lanes), FLOOR, F32)
    spans, base = [], 0
    for step in forward_steps(sizes):
        a, b = step[2:4]
        s = scores(kv, qs, sizes, step, slot)
        spans.append((base, base + s.shape[0]))
        base += s.shape[0]
        s_scr[spans[-1][0] : base, a:b] = s
        peak = over(peak, jnp.max(eights(s), axis=0), a, b, jnp.maximum)
    peak = jnp.max(peak, axis=0, keepdims=True) * SCALE2

    total = jnp.zeros((8, lanes), F32)
    out = jnp.zeros((D, lanes), F32)
    for (lo, hi), (kind, classes, a, b, _) in zip(spans, forward_steps(sizes)):
        rows, _, _, _, voff = pieces(sizes)[kind]
        p = jnp.exp2(s_scr[lo:hi, a:b] * SCALE2 - peak[:, a:b])
        kept = p.astype(BF16)
        if kind == 0:
            at = classes[0] * (hi - lo) // len(classes)
            p_prompt[at : at + hi - lo] = kept
        else:
            p_resp[:, (kind - 1) * (b - a) : kind * (b - a)] = kept
        part = mm(key_rows(kv, rows, voff, classes), kept, TN)
        out = over(out, part, a, b, jnp.add)
        total = over(total, jnp.sum(eights(p), axis=0), a, b, jnp.add)
    total = jnp.sum(total, axis=0, keepdims=True)
    stats[slot, 0:1] = peak
    stats[slot, 1:2] = total
    stats[slot, 2:3] = jnp.sum(out * gs[...].astype(F32).T, axis=0, keepdims=True)
    if slot == 0:
        stats[slot, 3:4, 0:D] = rest[0:1]
    spread(sizes, out * (1.0 / jnp.maximum(total, 1e-30)), part_out)


def combine_kernel(sizes, ways, copies, *refs):
    got, gs = refs[:ways], refs[ways : 2 * ways]
    info, shares, margin, scaled = refs[2 * ways :]
    tp = sizes[0]
    acc = jnp.zeros((1, 1), F32)
    shares[...] = jnp.zeros(shares.shape, F32)
    factors = []
    for i in range(ways):
        parts = [got[j][(i - j) % ways] for j in range(ways)]
        peak = functools.reduce(jnp.maximum, [p[0:1] for p in parts])
        scales = [jnp.exp2(p[0:1] - peak) for p in parts]
        total = sum(s * p[1:2] for s, p in zip(scales, parts))
        delta = sum(s * p[2:3] for s, p in zip(scales, parts)) / total
        factor = scales[0] / total
        factors.append(factor)
        info[i : i + 1] = delta * factor
        acc = acc + jnp.sum(delta[:, HEADS * tp :], axis=1, keepdims=True)
        if i == 0:
            for k in range(ways):
                j = -k % ways
                shares[k : k + 1] = scales[j] * parts[j][1:2] / total
    rest = sum(got[j][0, 3:4, 0:1] for j in range(ways)) / copies
    margin[...] = jnp.broadcast_to(BETA * (acc + rest), margin.shape)
    while len(factors) < 8:
        factors.append(jnp.zeros_like(factors[0]))
    cols = jnp.concatenate(factors, axis=0).T
    for i in range(ways):
        scaled[i] = (gs[i][...].astype(F32) * cols[:, i : i + 1]).astype(BF16)


def stamp(value, ref, at):
    row = lax.broadcasted_iota(jnp.int32, (16, D), 0)
    packed = jnp.zeros((16, D), F32)
    for i in range(3):
        part = value.astype(BF16).astype(F32)
        value = value - part
        packed = jnp.where(row == i, jnp.broadcast_to(part[0:1], (16, D)), packed)
    ref[at : at + 16] = packed.astype(BF16)


def stamped(ref, at):
    return jnp.sum(ref[at : at + 8].astype(F32), axis=0, keepdims=True)


def stamp_kernel(ways, *refs):
    margins, ins, outs = refs[:ways], refs[ways:-2], refs[-2:]
    total = sum(m[...] for m in margins)
    for out in outs:
        stamp(total, out, out.shape[0] - 16)


def backward_kernel(sizes, classes, ways, copies, *refs):
    refs = list(refs)

    def take(n):
        got = refs[:n]
        del refs[:n]
        return got

    kv = dict(zip(classes, take(len(classes))))
    qs = take(ways)
    take(2 * ways)
    gs, info = take(2)
    margins = take(copies) if copies else None
    *outs, acc = refs[-1 - len(classes) - 2 * ways :]
    outs, p_prompt, p_resp = outs[: -2 * ways], outs[-2 * ways : -ways], outs[-ways:]
    tp, tr, groups = sizes
    members = groups // CLASSES

    for slot in range(ways):
        for kind, _, a, b, _ in steps(sizes, [tuple(classes)], [tuple(classes)]):
            rows, _, _, koff, voff = pieces(sizes)[kind]
            keys = members * rows

            def put(off, value):
                value = value.reshape(len(classes), members, rows, D)
                at = (slice(None), slice(None), slice(off, off + rows), slice(None))
                acc[at] = value if slot == 0 else acc[at] + value

            ref = p_resp[slot] if kind else p_prompt[slot]
            side = slice((kind - 1) * (b - a), kind * (b - a)) if kind else slice(None)
            spans = [slice(e * keys, (e + 1) * keys) for e in classes]
            parts = [ref[span, side] for span in spans]
            p = parts[0] if len(parts) == 1 else jnp.concatenate(parts, axis=0)
            grad = gs[slot, a:b]
            dp = mm(key_rows(kv, rows, voff, classes), grad, NT)
            put(voff, mm(p, grad, NN))
            ds = (p.astype(F32) * (dp - info[slot : slot + 1, a:b])).astype(BF16)
            put(koff, mm(ds, qs[slot][a:b], NN))
            for i, span in enumerate(spans):
                ref[span, side] = ds[i * keys : (i + 1) * keys]
    for i, out in enumerate(outs):
        terms = acc[i].reshape(-1, D)
        out[0 : terms.shape[0]] = terms.astype(out.dtype)
        if margins:
            stamp(sum(m[...] for m in margins), out, terms.shape[0])


def queries_kernel(sizes, slots, *refs):
    kv, refs = refs[:CLASSES], refs[CLASSES:]
    n = len(slots)
    lanes = HEADS * (sizes[0] + 2 * sizes[1])
    for ds_prompt, ds_resp, end in zip(refs[:n], refs[n : 2 * n], refs[-n:]):
        dq = jnp.zeros((D, lanes), F32)
        for kind, classes, a, b, _ in forward_steps(sizes):
            rows, _, _, koff, _ = pieces(sizes)[kind]
            keys = sizes[2] // CLASSES * rows
            span = slice(classes[0] * keys, (classes[-1] + 1) * keys)
            side = slice((kind - 1) * (b - a), kind * (b - a)) if kind else slice(None)
            ds = (ds_resp if kind else ds_prompt)[span, side]
            dq = over(dq, mm(key_rows(kv, rows, koff, classes), ds, TN), a, b, jnp.add)
        spread(sizes, dq, end)


def middle_kernel(sizes, copies, shifts, mine, *refs):
    got, refs = refs[: CLASSES - 1], refs[CLASSES - 1 :]
    margins, outs = refs[:copies], refs[-len(shifts) :]
    tp, tr, groups = sizes
    n, members = 2 * tp + 4 * tr, groups // CLASSES
    at = lax.axis_index("prompt") // CLASSES
    total = sum(m[0:1] for m in margins) + sum(stamped(r, members * n) for r in got)
    for k, out in zip(shifts, outs):
        block = pl.ds(pl.multiple_of(lax.rem(at + k, members) * n, n), n)
        terms = mine[block] + sum(r[block].astype(F32) for r in got)
        out[0:n] = terms.astype(out.dtype)
        if k:
            stamp(jnp.broadcast_to(total, (8, D)), out, n)
        else:
            out[n : n + 8] = jnp.broadcast_to(total, (8, D))


def outputs_kernel(sizes, shares, *refs):
    *blocks, p_out, r_out = refs
    cols = shares[...].T
    for kind, (rows, lane, row, _, _) in enumerate(pieces(sizes)):
        for h in range(HEADS):
            at = lane + h * rows
            value = sum(
                o[row : row + rows, h * D : (h + 1) * D].astype(F32) * cols[at : at + rows, i : i + 1]
                for i, o in enumerate(blocks)
            ).astype(BF16)
            if kind == 0:
                p_out[:, h * D : (h + 1) * D] = value
            else:
                r_out[kind - 1, :, h * D : (h + 1) * D] = value


def final_kernel(sizes, ways, *refs):
    dqs, refs = refs[:ways], refs[ways:]
    tp, tr, groups = sizes
    n, members = 2 * tp + 4 * tr, groups // CLASSES
    *got, kept = refs[:members]
    refs = refs[members:]
    outs, (*held, sems) = refs[:5], refs[5:]
    p_dq, r_dq, p_dkv, r_dkv, loss = held
    margin = kept[n : n + 1] + sum(stamped(r, n) for r in got)
    z = -margin
    loss[...] = jnp.maximum(z, 0.0) + jnp.log1p(jnp.exp(-jnp.abs(z)))
    weight = (-BETA / (1.0 + jnp.exp(margin)))[:, 0:1]
    copies = [pltpu.make_async_copy(a, b, sems.at[i]) for i, (a, b) in enumerate(zip(held, outs))]
    copies[4].start()
    scaled = weight * SCALE

    def gathered(a, b):
        return (sum(r[a:b].astype(F32) for r in dqs) * scaled).astype(BF16)

    p_dq[...] = gathered(0, tp)
    copies[0].start()
    for s in range(2):
        r_dq[s] = gathered(tp + s * tr, tp + (s + 1) * tr)
    copies[1].start()

    def summed(a, b, scale):
        return ((kept[a:b] + sum(r[a:b].astype(F32) for r in got)) * scale).astype(BF16)

    for i, scale in enumerate((scaled, weight)):
        p_dkv[i] = summed(i * tp, (i + 1) * tp, scale)
        for s in range(2):
            a = 2 * tp + (2 * i + s) * tr
            r_dkv[i, s] = summed(a, a + tr, scale)
    copies[2].start()
    copies[3].start()
    for copy in copies:
        copy.wait()


VMEM = pl.BlockSpec(memory_space=pltpu.VMEM)
HBM = pl.BlockSpec(memory_space=pltpu.HBM)
sds = jax.ShapeDtypeStruct
held = pltpu.VMEM


def call(body, outs, ins, scratch=(), limit=32, aliases=None, flops=0, specs=None):
    def run(*args):
        args = [
            pltpu.with_memory_space_constraint(x, pltpu.VMEM if ins is VMEM else pltpu.HBM)
            for x in args
        ]
        return pl.pallas_call(
            body,
            out_shape=outs,
            in_specs=[ins] * len(args),
            out_specs=specs or jax.tree.map(lambda _: VMEM, outs),
            scratch_shapes=list(scratch),
            input_output_aliases=aliases or {},
            cost_estimate=pl.CostEstimate(flops=flops, bytes_accessed=0, transcendentals=0),
            compiler_params=pltpu.CompilerParams(vmem_limit_bytes=limit * 1024 * 1024),
        )(*args)

    return run


def shift(x, axis, by):
    n = lax.axis_size(axis)
    return lax.ppermute(x, axis, [(i, (i + by) % n) for i in range(n)])


def swap(x, other):
    return lax.ppermute(x, "prompt", [(i, i ^ other) for i in range(lax.axis_size("prompt"))])


def per_device(pq, pkv, rq, rkv, labels, logp, probe, pprobe):
    tp, tr = pq.shape[0], rq.shape[1]
    groups, ways = lax.axis_size("prompt"), lax.axis_size("resp")
    copies = lax.axis_size("dp")
    members = groups // CLASSES
    sizes = (tp, tr, groups)
    wide = HEADS * D
    n = 2 * tp + 4 * tr
    half = tp + 2 * tr
    lanes = HEADS * half

    qg, block, rest = call(
        functools.partial(pack_kernel, sizes),
        (held((2 * half, wide), BF16), held((n, D), BF16), held((8, D), F32)),
        HBM,
        [
            pltpu.VMEM(labels.shape, jnp.int32),
            pltpu.VMEM(logp.shape, F32),
            pltpu.VMEM(probe.shape, BF16),
            pltpu.SemaphoreType.DMA((13,)),
        ],
        limit=16,
    )(pq, pkv, rq, rkv, labels, logp, probe, pprobe)
    queries = [qg] + [shift(qg, "resp", j) for j in range(1, ways)]
    joined = call(join_kernel, held((members, n, D), BF16), VMEM, limit=16)(
        block, *[shift(block, "prompt", CLASSES * k) for k in range(1, members)],
        queries[1], queries[-1],
    )
    kv = [joined] + [swap(joined, e) for e in range(1, CLASSES)]

    order = [0, 1, ways - 1] + list(range(2, ways - 1))
    stats, kept = rest, {}
    scr = sum(len(c) * members * (tp if k == 0 else tr) for k, c, *_ in forward_steps(sizes))
    for slot in order:
        *made, stats = call(
            functools.partial(forward_kernel, sizes, slot),
            (
                held((lanes, D), BF16),
                held((lanes, D), BF16),
                held((half, wide), BF16),
                held((groups * tp, lanes), BF16),
                held((groups * tr, 2 * HEADS * tr), BF16),
                held((ways, 4, lanes), F32),
            ),
            VMEM,
            [pltpu.VMEM((scr, lanes), F32)],
            aliases={CLASSES + 1: 5} if slot else None,
            flops=2 * 2 * groups * half * lanes * D,
        )(*kv, queries[slot], stats)
        kept[slot] = made
    qs, gs, outs, p_prompt, p_resp = ([kept[j][i] for j in range(ways)] for i in range(5))
    all_stats = [stats, *[shift(stats, "resp", j) for j in range(1, ways)]]
    outs = [outs[0]] + [shift(outs[j], "resp", -j) for j in range(1, ways)]
    info, shares, margin, scaled = call(
        functools.partial(combine_kernel, sizes, ways, copies),
        (
            held((ways, lanes), F32),
            held((8, lanes), F32),
            held((8, D), F32),
            held((ways, lanes, D), BF16),
        ),
        VMEM,
        limit=16,
    )(*all_stats, *gs)
    margins = [margin] + [shift(margin, "dp", j) for j in range(1, copies)]

    message = held((members * n + 16, D), BF16)
    got = {}
    plans = [(3, 1), (2,), (0,)]
    for step, plan in enumerate(plans):
        first, last = step == 0, step == len(plans) - 1
        extra = margins if not first and not last else []
        ties = outs[1:2] if last else []
        at = len(plan) + ways
        results = call(
            functools.partial(backward_kernel, sizes, plan, ways, len(extra)),
            (
                *([held((members * n, D), F32)] if last else [message] * len(plan)),
                *[held((groups * tp, lanes), BF16)] * ways,
                *[held((groups * tr, 2 * HEADS * tr), BF16)] * ways,
            ),
            VMEM,
            [pltpu.VMEM((len(plan), members, n, D), F32)],
            aliases={at + i: len(plan) + i for i in range(2 * ways)},
            flops=4 * 2 * members * len(plan) * half * lanes * D * ways,
        )(*[kv[e] for e in plan], *qs, *p_prompt, *p_resp, scaled, info, *extra, *ties)
        messages, p_prompt, p_resp = results[: len(plan)], results[len(plan) : -ways], results[-ways:]
        if first:
            messages = call(
                functools.partial(stamp_kernel, copies),
                (message, message),
                VMEM,
                limit=16,
                aliases={copies: 0, copies + 1: 1},
            )(*margins, *messages)
        for e, m in zip(plan, messages):
            got[e] = m if last else swap(m, e)
    mine, dqs, late = got[0], {}, [[], outs[2:]]
    for slots in ((ways // 2, 1), tuple(j for j in range(ways) if j not in (ways // 2, 1))):
        made = call(
            functools.partial(queries_kernel, sizes, slots),
            (held((half, wide), BF16),) * len(slots),
            VMEM,
            flops=2 * groups * half * lanes * D * len(slots),
        )(*kv, *[p_prompt[j] for j in slots], *[p_resp[j] for j in slots], *late.pop())
        dqs.update(zip(slots, made))
    dqs = [dqs[0]] + [shift(dqs[j], "resp", -j) for j in range(1, ways)]
    terms = []
    for shifts, ties in (((members // 2, 1), []), ((members - 1, 0), [dqs[ways // 2]])):
        sends = call(
            functools.partial(middle_kernel, sizes, copies, shifts),
            tuple(held((n + 16, D), BF16) if k else held((n + 8, D), F32) for k in shifts),
            VMEM,
            limit=16,
        )(mine, *[got[e] for e in range(1, CLASSES)], *margins, *ties)
        for k, x in zip(shifts, sends):
            terms.append(shift(x, "prompt", CLASSES * k) if k else x)

    p_out, r_out = call(
        functools.partial(outputs_kernel, sizes),
        (sds(pq.shape, BF16), sds(rq.shape, BF16)),
        VMEM,
        limit=16,
    )(shares, *outs)
    results = [
        (pq.shape, BF16),
        (rq.shape, BF16),
        (pkv.shape, BF16),
        (rkv.shape, BF16),
        ((1, D), F32),
    ]
    p_dq, r_dq, p_dkv, r_dkv, loss = call(
        functools.partial(final_kernel, sizes, ways),
        tuple(sds(*o) for o in results),
        VMEM,
        [pltpu.VMEM(*o) for o in results] + [pltpu.SemaphoreType.DMA((5,))],
        limit=16,
        specs=(HBM,) * 5,
    )(*dqs, *terms)
    return (p_out, r_out, p_dq, r_dq, p_dkv, r_dkv, loss[0, 0])


def solution(mesh):
    placed = (
        P(("prompt", "resp"), "dp"),
        P(None, ("prompt", "resp"), "dp"),
        P(None, ("prompt", "resp"), "dp"),
        P(None, None, ("prompt", "resp"), "dp"),
        P(None, ("prompt", "resp")),
        P(None, ("prompt", "resp")),
        P(None, ("prompt", "resp"), "dp"),
        P(("prompt", "resp"), "dp"),
    )
    return jax.shard_map(
        per_device,
        mesh=mesh,
        in_specs=placed,
        out_specs=(
            P(("prompt", "resp"), "dp"),
            P(None, ("prompt", "resp"), "dp"),
            P(("prompt", "resp"), "dp"),
            P(None, ("prompt", "resp"), "dp"),
            P(None, ("prompt", "resp"), "dp"),
            P(None, None, ("prompt", "resp"), "dp"),
            P(),
        ),
        check_vma=False,
    )
```
